128 devices in a mesh: ctx: 32 (over z, x, core), user: 4 (over y).
Axes of the slice: x: 4, y: 4, z: 4, core: 2. Of those that a mesh axis runs over, the one named last changes fastest.
Arguments:
- robe_array: bfloat16 [524288, 128], P(('ctx', 'user')), may hold values from -6 to 6
- block_owner: int32 [4, 32768, 4], P('user', 'ctx'), may hold values from 0 to 127, all different within a row; in each aligned block of 1024 rows (0 to 1023, 1024 to 2047, ..., all dimensions but the last counted through in order) at most 80 rows name the same one
- block_slot: int32 [4, 32768, 4], P('user', 'ctx'), may hold values from 0 to 4095
- w_query: bfloat16 [512, 512], replicated, may hold values from -0.25 to 0.25
- w_key: bfloat16 [512, 512], replicated, may hold values from -0.25 to 0.25
- w_value: bfloat16 [512, 512], replicated, may hold values from -0.25 to 0.25
- w_gate: bfloat16 [512, 512], replicated, may hold values from -0.25 to 0.25
- w_output: bfloat16 [512, 512], replicated, may hold values from -0.25 to 0.25
- head_gain: float32 [512], replicated, may hold values from 0.1 to 1.9
Outputs:
- encoded: bfloat16 [4, 32768, 512], P('user', 'ctx')
The draws below stay inside these ranges and needn't reach their ends.
Inputs may be any that keep to these rules, and one draw needn't show every extreme that they name: `block_owner`: the four owners of one position differ; over the positions of one device no owner is named more than 80 times, a bound that some block reaches.
All inputs are finite; a program needn't handle non-finite values.
Results may differ from the reference program's by a relative error of at most 0.015.
Values may be sent and summed in bfloat16 or wider, within the bound.
A program may use at most 128 MiB of HBM per device.

```python
import math
import jax
import jax.numpy as jnp
import numpy as np
from jax import lax

BLOCK = 128
PARTS_SIZE = 4
D = 512
HEADS = 4
HEAD = 128
POS_DEV = 1024
BLOCKS_DEV = 4096
USERS = 4
L = 32768
CAP = 80
N_CTX = 32
N_USER = 4


def set_ends(entries, rng, low, largest):
    extent = entries.shape
    place = [jax.random.randint(jax.random.fold_in(rng, axis), (), 0, extent[axis]) for axis in range(len(extent))]
    entries = entries.at[tuple(place)].set(low)
    longest = extent.index(max(extent))
    place[longest] = (place[longest] + 1) % extent[longest]
    return entries.at[tuple(place)].set(largest)


def steps_of(rng, extent, cuts, low, top_value):
    def one(axis_at, shards_of):
        draws = jax.random.uniform(jax.random.fold_in(jax.random.fold_in(rng, 6), axis_at), (shards_of,), jnp.float32, low / len(cuts), top_value / len(cuts))
        return jnp.repeat(jnp.exp(draws), extent[axis_at] // shards_of).reshape((-1,) + (1,) * (len(extent) - axis_at - 1))

    level = one(*cuts[0])
    for cut in cuts[1:]:
        level = level * one(*cut)
    return level


def assign_block(rng, own, number, rows, number_of, top, most, lean):
    sequence = jax.random.permutation(rng, number_of)
    crowded, ordinary = portions_of(number_of, rows * top, most, lean, True), portions_of(number_of, rows * top, most, lean, False)
    places = jnp.arange(number_of)

    def named(lengths, turn):
        used = int((lengths > 0).sum())
        fixed = max(1, used // 4)
        moved = fixed + (places - fixed + turn * (used - fixed)) % max(1, number_of - fixed)
        return jnp.zeros((number_of,), jnp.int32).at[sequence[jnp.where(places < fixed, places, moved)]].set(jnp.asarray(lengths, jnp.int32))

    lengths = jnp.where(number % 4 == 0, named(crowded, number // 4), named(ordinary, number - number // 4 - 1))
    mixed = jax.random.permutation(jax.random.fold_in(own, 3), number_of)
    donor, receiver = mixed[0:number_of // 2 * 2:2], mixed[1:number_of // 2 * 2:2]
    room = jnp.minimum(lengths[donor] - 1, most - lengths[receiver]) // 2
    room = jnp.where((donor == sequence[0]) | (receiver == sequence[0]) | (lengths[receiver] == 0), 0, jnp.maximum(room, 0))
    moved = jax.random.randint(jax.random.fold_in(own, 4), (number_of // 2,), 0, 1 << 20) % (room + 1)
    lengths = lengths.at[donor].add(-moved).at[receiver].add(moved)
    labels = jnp.searchsorted(jnp.cumsum(lengths), jnp.arange(rows * top), side="right").astype(jnp.int32)
    grid = labels.reshape(top, rows).T
    grid = grid[jax.random.permutation(jax.random.fold_in(own, 1), rows)]
    turn = jax.random.randint(jax.random.fold_in(own, 2), (rows, 1), 0, top)
    return jnp.take_along_axis(grid, (jnp.arange(top)[None, :] + turn) % top, axis=1)


def portions_of(count, total, reach, skew, full):
    portions = [(1 << 20) // math.isqrt(rank ** skew) + 1 for rank in range(1, count + 1)]
    largest = reach if full else min(reach, max(-(-total // count), total * portions[0] // sum(portions)))
    least = 1 if total - largest >= count - 1 else 0
    holding, rest = [largest] + [least] * (count - 1), total - largest - least * (count - 1)
    while rest > 0:
        movable = [i for i in range(1, count) if holding[i] < largest] or [i for i in range(1, count) if holding[i] < reach]
        mass, remaining = sum([portions[i] for i in movable]), rest
        for i in movable:
            more = min(reach - holding[i], max(1, remaining * portions[i] // mass), rest)
            holding[i] = holding[i] + more
            rest = rest - more
    return np.array(holding)


def normal_values(own_key, shape, deviation, most, shards=(), kind=jnp.bfloat16):
    entries = jax.random.normal(own_key, shape, jnp.float32) * deviation
    if len(shards) > 0:
        entries = steps_of(own_key, shape, shards, -0.22, 0.18) * entries
    return jnp.clip(entries, min=-most, max=most).astype(kind)


def setup_inputs(seed: int = 0) -> dict:
    keys = jax.random.split(jax.random.key(seed), 10)
    robe_array = normal_values(keys[0], (N_CTX * N_USER * BLOCKS_DEV, BLOCK), 1.0, 6.0, ((0, 128),))
    block_owner_keys = jax.random.split(jax.random.fold_in(keys[1], 1), USERS * L // POS_DEV)
    block_owner_turns = jax.random.permutation(jax.random.fold_in(keys[1], 3), USERS * L // POS_DEV)
    block_owner = jax.vmap(lambda own, number: assign_block(jax.random.fold_in(keys[1], 2), own, number, POS_DEV, N_CTX * N_USER, PARTS_SIZE, CAP, 1))(block_owner_keys, block_owner_turns).reshape((USERS, L, PARTS_SIZE))
    block_slot = set_ends(jax.random.randint(keys[2], (USERS, L, PARTS_SIZE), 0, BLOCKS_DEV), jax.random.fold_in(keys[2], 1), 0, BLOCKS_DEV - 1).astype(jnp.int32)
    w_query = normal_values(keys[3], (D, D), D ** -0.5, 0.25)
    w_key = normal_values(keys[4], (D, D), D ** -0.5, 0.25)
    w_value = normal_values(keys[5], (D, D), D ** -0.5, 0.25)
    w_gate = normal_values(keys[6], (D, D), D ** -0.5, 0.25)
    w_output = normal_values(keys[7], (D, D), D ** -0.5, 0.25)
    head_gain = jnp.clip(1.0 + 0.18 * jax.random.normal(keys[8], (D,), jnp.float32), 0.1, 1.9)
    return {"robe_array": robe_array, "block_owner": block_owner, "block_slot": block_slot, "w_query": w_query, "w_key": w_key, "w_value": w_value, "w_gate": w_gate, "w_output": w_output, "head_gain": head_gain}


def attend(queries, keys_in, values_in):
    length = queries.shape[0]
    block_rows = min(512, length)
    count = length // block_rows
    qblocks = (jax.nn.elu(queries.astype(jnp.float32)) + 1.0).reshape(count, block_rows, HEADS, HEAD)
    kblocks = (jax.nn.elu(keys_in.astype(jnp.float32)) + 1.0).reshape(count, block_rows, HEADS, HEAD)
    vblocks = values_in.astype(jnp.float32).reshape(count, block_rows, HEADS, HEAD)
    causal = jnp.tril(jnp.ones((block_rows, block_rows), jnp.float32))

    def advance(state, items):
        qpart, kpart, vpart = items
        scores = jnp.einsum('the,she->hts', qpart, kpart, precision=lax.Precision.HIGHEST) * causal[None]
        local = jnp.einsum('hts,she->the', scores, vpart, precision=lax.Precision.HIGHEST)
        carried = jnp.einsum('the,hef->thf', qpart, state, precision=lax.Precision.HIGHEST)
        state = state + jnp.einsum('she,shf->hef', kpart, vpart, precision=lax.Precision.HIGHEST)
        return (state, local + carried)
    start = jnp.zeros((HEADS, HEAD, HEAD), jnp.float32)
    _, mixed = lax.scan(advance, start, (qblocks, kblocks, vblocks))
    return mixed.reshape(length, HEADS, HEAD)

def reference(robe_array, block_owner, block_slot, w_query, w_key, w_value, w_gate, w_output, head_gain):

    def one_user(items):
        owners, slots = items
        index = (owners * BLOCKS_DEV + slots).astype(jnp.int32)
        embed = robe_array[index].reshape(L, D)
        queries = jnp.dot(embed, w_query, preferred_element_type=jnp.float32).astype(jnp.bfloat16)
        keys_in = jnp.dot(embed, w_key, preferred_element_type=jnp.float32).astype(jnp.bfloat16)
        values_in = jnp.dot(embed, w_value, preferred_element_type=jnp.float32).astype(jnp.bfloat16)
        gates = jnp.dot(embed, w_gate, preferred_element_type=jnp.float32).astype(jnp.bfloat16)
        mixed = attend(queries.reshape(L, HEADS, HEAD), keys_in.reshape(L, HEADS, HEAD), values_in.reshape(L, HEADS, HEAD))
        mean_square = lax.optimization_barrier(jnp.mean(mixed * mixed, axis=-1, keepdims=True))
        normed = mixed / jnp.sqrt(mean_square + 1e-06) * head_gain.reshape(HEADS, HEAD)[None]
        gated = (normed.reshape(L, D) * jax.nn.silu(gates.astype(jnp.float32))).astype(jnp.bfloat16)
        return jnp.dot(gated, w_output, preferred_element_type=jnp.float32).astype(jnp.bfloat16)
    return lax.map(one_user, (block_owner, block_slot))
```

```python
import jax
import jax.numpy as jnp
from jax import lax
from jax.experimental import pallas as pl
from jax.experimental.pallas import tpu as pltpu
from jax.sharding import PartitionSpec as P

MESH = pl.DeviceIdType.MESH
HEADS = 4
HEAD = 128
CAP = 80
GROUP = 16
CHUNK = 256
F32 = jnp.float32
BF16 = jnp.bfloat16


def moved(k, sign):
    c, y = lax.axis_index("ctx"), lax.axis_index("user")
    core, r = k % 2, k // 2
    a, b, e = r % 4, (r // 4) % 4, r // 16
    z = (c // 8 + 8 + sign * (a + b + e)) % 4
    x = ((c // 2) % 4 + 8 + sign * a) % 4
    u = (y + 8 + sign * (a + b)) % 4
    return z * 8 + x * 2 + (c + core) % 2, u


def rank_kernel(own_ref, slot_ref, req, index_ref):
    devices = req.shape[0]
    parts, positions = own_ref.shape
    device_row = lax.broadcasted_iota(jnp.int32, (devices, CHUNK), 0)
    rank_row = lax.broadcasted_iota(jnp.int32, (128, CHUNK), 0)
    upper = (
        lax.broadcasted_iota(jnp.int32, (CHUNK, CHUNK), 0)
        <= lax.broadcasted_iota(jnp.int32, (CHUNK, CHUNK), 1)
    ).astype(F32).astype(BF16)
    before = jnp.zeros((devices, 1), F32)
    total = jnp.zeros((devices, 256), F32)
    for j in range(parts):
        for p in range(0, positions, CHUNK):
            own = own_ref[j : j + 1, p : p + CHUNK]
            slot = slot_ref[j : j + 1, p : p + CHUNK]
            named = device_row == own
            hot = jnp.where(named, 1.0, 0.0).astype(BF16)
            count = jnp.dot(hot, upper, preferred_element_type=F32) + before
            before = count[:, CHUNK - 1 :]
            rank = jnp.sum(jnp.where(named, count, 0.0), axis=0, keepdims=True).astype(jnp.int32) - 1
            index_ref[j : j + 1, p : p + CHUNK] = own * CAP + rank
            at_rank = rank_row == rank
            high = jnp.where(at_rank, (slot // 64).astype(F32), 0.0).astype(BF16)
            low = jnp.where(at_rank, (slot % 64).astype(F32), 0.0).astype(BF16)
            total += lax.dot_general(
                hot, jnp.concatenate([high, low], axis=0), (((1,), (1,)), ((), ())),
                preferred_element_type=F32,
            )
    req[...] = (total[:, :128] * 64.0 + total[:, 128:]).astype(jnp.int32)


def rank(owner, slot):
    devices = lax.axis_size("ctx") * lax.axis_size("user")
    vmem = pl.BlockSpec(memory_space=pltpu.VMEM)
    return pl.pallas_call(
        rank_kernel,
        out_shape=(
            jax.ShapeDtypeStruct((devices, 128), jnp.int32),
            jax.ShapeDtypeStruct(owner.shape, jnp.int32),
        ),
        in_specs=[vmem] * 2,
        out_specs=(vmem, vmem),
        name="rank",
    )(owner, slot)


def fetch_kernel(
    req, table_ref, rows_ref,
    landed, arrived, table, gathered, send, recv,
    req_out, req_in, own_sem, row_out, row_in,
):
    devices = send.shape[0]
    groups = devices // GROUP
    me = lax.axis_index("ctx") * lax.axis_size("user") + lax.axis_index("user")
    barrier = pltpu.get_barrier_semaphore()

    def greet(k, carry):
        pl.semaphore_signal(barrier, inc=1, device_id=moved(k, 1), device_id_type=MESH)
        return carry

    lax.fori_loop(1, devices, greet, 0)

    def widen(k, carry):
        s = pl.ds(pl.multiple_of(k * 256, 256), 256)
        table[s] = table_ref[s].astype(F32)
        return carry

    lax.fori_loop(0, table.shape[0] // 256, widen, 0)

    pl.semaphore_wait(barrier, devices - 1)

    def ask(k, carry):
        ctx, user = moved(k, 1)
        owner = ctx * lax.axis_size("user") + user
        pltpu.make_async_remote_copy(
            req.at[pl.ds(owner, 1)], landed.at[pl.ds(me, 1)], req_out, req_in.at[k // GROUP],
            device_id=(ctx, user), device_id_type=MESH,
        ).start()
        return carry

    lax.fori_loop(1, devices, ask, 0)
    landed[pl.ds(me, 1)] = req[pl.ds(me, 1)]
    for g in range(groups):
        some = req.at[pl.ds(0, GROUP - (1 if g == 0 else 0))]
        pltpu.make_async_copy(some, some, req_in.at[g]).wait()
    mine = pltpu.make_async_copy(landed, arrived, own_sem)
    mine.start()
    mine.wait()

    def gather(asker):
        for i in range(CAP):
            gathered[pl.ds(i, 1)] = table[pl.ds(arrived[asker, i], 1)]
        return gathered[...].astype(BF16)

    def answer(k, carry):
        ctx, user = moved(k, -1)
        asker = ctx * lax.axis_size("user") + user
        send[asker] = gather(asker)
        pltpu.make_async_remote_copy(
            send.at[asker], recv.at[me], row_out, row_in.at[k // GROUP],
            device_id=(ctx, user), device_id_type=MESH,
        ).start()
        return carry

    for g in range(groups):
        first = 1 if g == 0 else 0
        lax.fori_loop(g * GROUP + first, (g + 1) * GROUP, answer, 0)
    recv[me] = gather(me)

    def unpack(k, carry):
        ctx, user = moved(k, 1)
        owner = ctx * lax.axis_size("user") + user
        rows_ref[owner] = recv[owner].astype(F32)
        return carry

    for g in range(groups):
        first = 1 if g == 0 else 0
        some = recv.at[pl.ds(0, GROUP - first)]
        pltpu.make_async_copy(some, some, row_in.at[g]).wait()
        lax.fori_loop(g * GROUP, (g + 1) * GROUP, unpack, 0)
    some = req.at[pl.ds(0, devices - 1)]
    pltpu.make_async_copy(some, some, req_out).wait()
    some = send.at[pl.ds(0, devices - 1)]
    pltpu.make_async_copy(some, some, row_out).wait()


def fetch(requests, table):
    devices = lax.axis_size("ctx") * lax.axis_size("user")
    vmem = pl.BlockSpec(memory_space=pltpu.VMEM)
    return pl.pallas_call(
        fetch_kernel,
        out_shape=jax.ShapeDtypeStruct((devices, CAP, table.shape[1]), F32),
        in_specs=[vmem] * 2,
        out_specs=vmem,
        scratch_shapes=[
            pltpu.VMEM((devices, 128), jnp.int32),
            pltpu.SMEM((devices, 128), jnp.int32),
            pltpu.VMEM(table.shape, F32),
            pltpu.VMEM((CAP, table.shape[1]), F32),
            pltpu.VMEM((devices, CAP, table.shape[1]), BF16),
            pltpu.VMEM((devices, CAP, table.shape[1]), BF16),
            pltpu.SemaphoreType.DMA,
            pltpu.SemaphoreType.DMA((devices // GROUP,)),
            pltpu.SemaphoreType.DMA,
            pltpu.SemaphoreType.DMA,
            pltpu.SemaphoreType.DMA((devices // GROUP,)),
        ],
        compiler_params=pltpu.CompilerParams(
            collective_id=0, has_side_effects=True, vmem_limit_bytes=48 << 20
        ),
        name="fetch",
    )(requests, table)


def attend_kernel(
    index_ref, rows_ref, wq_ref, wk_ref, wv_ref, wg_ref, wo_ref, gain_ref, out_ref,
    embed, fq, fk, values, gates, intra, state, packed, from_each, earlier, entering,
    out_a, in_a, out_b, in_b,
):
    ctx_size = lax.axis_size("ctx")
    ctx, user = lax.axis_index("ctx"), lax.axis_index("user")
    barrier = pltpu.get_barrier_semaphore()

    def greet(k, carry):
        pl.semaphore_signal(
            barrier, inc=1, device_id=((ctx + k) % ctx_size, user), device_id_type=MESH
        )
        return carry

    lax.fori_loop(1, ctx_size, greet, 0)

    parts, positions = index_ref.shape
    chunks = positions // CHUNK

    def collect(b, carry):
        for i in range(16):
            for j in range(parts):
                embed[j, pl.ds(b * 16 + i, 1)] = rows_ref[pl.ds(index_ref[j, b * 16 + i], 1)]
        return carry

    lax.fori_loop(0, positions // 16, collect, 0)

    def feature(v):
        v = v.astype(BF16).astype(F32)
        return jnp.where(v > 0, v + 1.0, jnp.exp(jnp.minimum(v, 0.0))).astype(BF16)

    running = [jnp.zeros((HEAD, HEAD), F32)] * HEADS
    for c in range(chunks):
        at = pl.ds(c * CHUNK, CHUNK)
        e = jnp.concatenate([embed[j, at] for j in range(parts)], axis=1).astype(BF16)
        k = feature(jnp.dot(e, wk_ref[...], preferred_element_type=F32))
        v = jnp.dot(e, wv_ref[...], preferred_element_type=F32).astype(BF16)
        fk[at] = k
        values[at] = v
        for h in range(HEADS):
            s = slice(h * HEAD, (h + 1) * HEAD)
            state[c, h] = running[h]
            running[h] = running[h] + lax.dot_general(
                k[:, s], v[:, s], (((0,), (0,)), ((), ())), preferred_element_type=F32
            )
    rows = HEADS * HEAD // ctx_size
    for h in range(HEADS):
        for i in range(HEAD // rows):
            packed[h * (HEAD // rows) + i] = running[h][i * rows : (i + 1) * rows].astype(BF16)

    pl.semaphore_wait(barrier, ctx_size - 1)

    def part_out(k, carry):
        other = (ctx + k) % ctx_size
        pltpu.make_async_remote_copy(
            packed.at[other], from_each.at[ctx], out_a, in_a,
            device_id=(other, user), device_id_type=MESH,
        ).start()
        return carry

    lax.fori_loop(1, ctx_size, part_out, 0)
    from_each[ctx] = packed[ctx]

    causal = lax.broadcasted_iota(jnp.int32, (CHUNK, CHUNK), 0) >= lax.broadcasted_iota(
        jnp.int32, (CHUNK, CHUNK), 1
    )

    def local(c):
        at = pl.ds(c * CHUNK, CHUNK)
        e = jnp.concatenate([embed[j, at] for j in range(parts)], axis=1).astype(BF16)
        q = feature(jnp.dot(e, wq_ref[...], preferred_element_type=F32))
        fq[at] = q
        gates[at] = jnp.dot(e, wg_ref[...], preferred_element_type=F32).astype(BF16)
        for h in range(HEADS):
            s = slice(h * HEAD, (h + 1) * HEAD)
            scores = lax.dot_general(
                q[:, s], fk[at, s], (((1,), (1,)), ((), ())), preferred_element_type=F32
            )
            scores = jnp.where(causal, scores, 0.0).astype(BF16)
            intra[at, s] = jnp.dot(scores, values[at, s], preferred_element_type=F32)

    for c in range(chunks // 2):
        local(c)

    some = packed.at[pl.ds(0, ctx_size - 1)]
    pltpu.make_async_copy(some, some, in_a).wait()
    pltpu.make_async_copy(some, some, out_a).wait()
    sofar = jnp.zeros((rows, HEAD), F32)
    for i in range(ctx_size):
        earlier[i] = sofar.astype(BF16)
        sofar = sofar + from_each[i].astype(F32)

    def part_back(k, carry):
        other = (ctx + k) % ctx_size
        pltpu.make_async_remote_copy(
            earlier.at[other], entering.at[ctx], out_b, in_b,
            device_id=(other, user), device_id_type=MESH,
        ).start()
        return carry

    lax.fori_loop(1, ctx_size, part_back, 0)
    entering[ctx] = earlier[ctx]

    for c in range(chunks // 2, chunks):
        local(c)

    pltpu.make_async_copy(some, some, in_b).wait()
    pltpu.make_async_copy(some, some, out_b).wait()

    for c in range(chunks):
        at = pl.ds(c * CHUNK, CHUNK)
        heads = []
        for h in range(HEADS):
            s = slice(h * HEAD, (h + 1) * HEAD)
            n = HEAD // rows
            came = entering[h * n : (h + 1) * n].reshape(HEAD, HEAD).astype(F32)
            within = (state[c, h] + came).astype(BF16)
            mixed = intra[at, s] + jnp.dot(fq[at, s], within, preferred_element_type=F32)
            square = jnp.mean(mixed * mixed, axis=1, keepdims=True)
            gate = gates[at, s].astype(F32)
            normed = mixed * lax.rsqrt(square + 1e-6) * gain_ref[:, s]
            heads.append((normed * (gate / (1.0 + jnp.exp(-gate)))).astype(BF16))
        out_ref[at] = jnp.dot(
            jnp.concatenate(heads, axis=1), wo_ref[...], preferred_element_type=F32
        ).astype(BF16)


def attend(index, rows, wq, wk, wv, wg, wo, gain):
    ctx_size = lax.axis_size("ctx")
    parts, positions = index.shape
    width = wq.shape[1]
    vmem = pl.BlockSpec(memory_space=pltpu.VMEM)
    piece = pltpu.VMEM((ctx_size, HEADS * HEAD // ctx_size, HEAD), BF16)
    return pl.pallas_call(
        attend_kernel,
        out_shape=jax.ShapeDtypeStruct((positions, width), BF16),
        in_specs=[pl.BlockSpec(memory_space=pltpu.SMEM)] + [vmem] * 7,
        out_specs=vmem,
        scratch_shapes=[
            pltpu.VMEM((parts, positions, width // parts), F32),
            pltpu.VMEM((positions, width), BF16),
            pltpu.VMEM((positions, width), BF16),
            pltpu.VMEM((positions, width), BF16),
            pltpu.VMEM((positions, width), BF16),
            pltpu.VMEM((positions, width), F32),
            pltpu.VMEM((positions // CHUNK, HEADS, HEAD, HEAD), F32),
            piece, piece, piece, piece,
            pltpu.SemaphoreType.DMA,
            pltpu.SemaphoreType.DMA,
            pltpu.SemaphoreType.DMA,
            pltpu.SemaphoreType.DMA,
        ],
        compiler_params=pltpu.CompilerParams(
            collective_id=1, has_side_effects=True, vmem_limit_bytes=48 << 20
        ),
        name="attend",
    )(index, rows, wq, wk, wv, wg, wo, gain)


def shards(
    robe_array, block_owner, block_slot, w_query, w_key, w_value, w_gate, w_output, head_gain
):
    owner = jnp.swapaxes(block_owner[0], 0, 1)
    slot = jnp.swapaxes(block_slot[0], 0, 1)
    requests, index = rank(owner, slot)
    rows = fetch(requests, robe_array)
    encoded = attend(
        index, rows.reshape(-1, rows.shape[2]), w_query, w_key, w_value, w_gate, w_output,
        head_gain.reshape(1, -1),
    )
    return encoded[None]


def solution(mesh):
    return jax.shard_map(
        shards,
        mesh=mesh,
        in_specs=(
            P(("ctx", "user"), None),
            P("user", "ctx", None),
            P("user", "ctx", None),
            P(),
            P(),
            P(),
            P(),
            P(),
            P(),
        ),
        out_specs=P("user", "ctx", None),
        check_vma=False,
    )
```

```python
import jax
import jax.numpy as jnp
from jax import lax
from jax.experimental import pallas as pl
from jax.experimental.pallas import tpu as pltpu
from jax.sharding import PartitionSpec as P

MESH = pl.DeviceIdType.MESH
HEADS = 4
HEAD = 128
CAP = 80
GROUP = 16
CHUNK = 256
F32 = jnp.float32
BF16 = jnp.bfloat16


def moved(k, sign):
    c, y = lax.axis_index("ctx"), lax.axis_index("user")
    core, r = k % 2, k // 2
    a, b, e = r % 4, (r // 4) % 4, r // 16
    z = (c // 8 + 8 + sign * (a + b + e)) % 4
    x = ((c // 2) % 4 + 8 + sign * a) % 4
    u = (y + 8 + sign * (a + b)) % 4
    return z * 8 + x * 2 + (c + core) % 2, u


def fetch_kernel(
    own_ref, slot_ref, table_hbm, rows_ref, index_ref,
    req, landed, arrived, packed, table, gathered, send, recv,
    table_in, req_out, req_in, read_in, row_out, row_in,
):
    devices = send.shape[0]
    groups = devices // GROUP
    users = lax.axis_size("user")
    me = lax.axis_index("ctx") * users + lax.axis_index("user")
    barrier = pltpu.get_barrier_semaphore()

    load = pltpu.make_async_copy(table_hbm, packed, table_in)
    load.start()

    parts, positions = own_ref.shape
    device_row = lax.broadcasted_iota(jnp.int32, (devices, CHUNK), 0)
    rank_row = lax.broadcasted_iota(jnp.int32, (128, CHUNK), 0)
    upper = jnp.where(
        lax.broadcasted_iota(jnp.int32, (CHUNK, CHUNK), 0)
        <= lax.broadcasted_iota(jnp.int32, (CHUNK, CHUNK), 1),
        1.0, 0.0,
    ).astype(BF16)
    before = jnp.zeros((devices, 1), F32)
    greeted, greetings = 0, devices * CHUNK // (parts * positions)
    total = jnp.zeros((devices, 256), F32)
    for j in range(parts):
        for p in range(0, positions, CHUNK):
            for k in range(greeted, greeted + greetings):
                if k > 0:
                    pl.semaphore_signal(
                        barrier, inc=1, device_id=moved(k, 1), device_id_type=MESH
                    )
            greeted += greetings
            own = own_ref[j : j + 1, p : p + CHUNK]
            slot = slot_ref[j : j + 1, p : p + CHUNK]
            named = device_row == own
            hot = jnp.where(named, 1.0, 0.0).astype(BF16)
            count = jnp.dot(hot, upper, preferred_element_type=F32) + before
            before = count[:, CHUNK - 1 :]
            rank = jnp.sum(jnp.where(named, count, 0.0), axis=0, keepdims=True).astype(jnp.int32) - 1
            index_ref[j : j + 1, p : p + CHUNK] = own * CAP + rank
            at_rank = rank_row == rank
            high = jnp.where(at_rank, (slot >> 6).astype(F32), 0.0).astype(BF16)
            low = jnp.where(at_rank, (slot & 63).astype(F32), 0.0).astype(BF16)
            total += lax.dot_general(
                hot, jnp.concatenate([high, low], axis=0), (((1,), (1,)), ((), ())),
                preferred_element_type=F32,
            )
    asked = (total[:, :128] * 64.0 + total[:, 128:]).astype(jnp.int32)
    req[...] = jnp.minimum(jnp.maximum(asked, 0), table.shape[0] - 1)
    landed[pl.ds(0, 1)] = req[pl.ds(me, 1)]
    load.wait()

    def widen(k, carry):
        s = pl.ds(pl.multiple_of(k * 256, 256), 256)
        table[s] = packed[s].astype(F32)
        return carry

    lax.fori_loop(0, table.shape[0] // 256, widen, 0)
    pl.semaphore_wait(barrier, devices - 1)

    def ask(k, carry):
        ctx, user = moved(k, 1)
        pltpu.make_async_remote_copy(
            req.at[pl.ds(ctx * users + user, 1)], landed.at[pl.ds(k, 1)], req_out,
            req_in.at[k // GROUP], device_id=(ctx, user), device_id_type=MESH,
        ).start()
        return carry

    def gather(k):
        for i in range(CAP):
            gathered[pl.ds(i, 1)] = table[pl.ds(arrived[k, i], 1)]
        return gathered[...].astype(BF16)

    def answer(k, carry):
        ctx, user = moved(k, -1)
        send[k] = gather(k)
        pltpu.make_async_remote_copy(
            send.at[k], recv.at[me], row_out, row_in.at[k // GROUP],
            device_id=(ctx, user), device_id_type=MESH,
        ).start()
        return carry

    def read(g):
        some = landed.at[pl.ds(g * GROUP, GROUP)]
        return pltpu.make_async_copy(some, arrived.at[pl.ds(g * GROUP, GROUP)], read_in.at[g])

    def come(g):
        some = req.at[pl.ds(0, GROUP - (1 if g == 0 else 0))]
        pltpu.make_async_copy(some, some, req_in.at[g]).wait()
        read(g).start()

    def asks(g):
        lax.fori_loop(g * GROUP + (1 if g == 0 else 0), (g + 1) * GROUP, ask, 0, unroll=True)

    for g in range(groups):
        asks(g)
    come(0)
    for g in range(groups):
        if g + 1 < groups:
            come(g + 1)
        read(g).wait()
        lax.fori_loop(g * GROUP + (1 if g == 0 else 0), (g + 1) * GROUP, answer, 0)
    recv[me] = gather(0)

    def unpack(k, carry):
        ctx, user = moved(k, 1)
        owner = ctx * users + user
        rows_ref[owner] = recv[owner].astype(F32)
        return carry

    for g in range(groups):
        some = recv.at[pl.ds(0, GROUP - (1 if g == 0 else 0))]
        pltpu.make_async_copy(some, some, row_in.at[g]).wait()
        lax.fori_loop(g * GROUP, (g + 1) * GROUP, unpack, 0)
    some = req.at[pl.ds(0, devices - 1)]
    pltpu.make_async_copy(some, some, req_out).wait()
    some = send.at[pl.ds(0, devices - 1)]
    pltpu.make_async_copy(some, some, row_out).wait()


def fetch(owner, slot, table):
    devices = lax.axis_size("ctx") * lax.axis_size("user")
    groups = devices // GROUP
    vmem = pl.BlockSpec(memory_space=pltpu.VMEM)
    return pl.pallas_call(
        fetch_kernel,
        out_shape=(
            jax.ShapeDtypeStruct((devices, CAP, table.shape[1]), F32),
            jax.ShapeDtypeStruct(owner.shape, jnp.int32),
        ),
        in_specs=[vmem, vmem, pl.BlockSpec(memory_space=pl.ANY)],
        out_specs=(vmem, vmem),
        scratch_shapes=[
            pltpu.VMEM((devices, 128), jnp.int32),
            pltpu.VMEM((devices, 128), jnp.int32),
            pltpu.SMEM((devices, 128), jnp.int32),
            pltpu.VMEM(table.shape, BF16),
            pltpu.VMEM(table.shape, F32),
            pltpu.VMEM((CAP, table.shape[1]), F32),
            pltpu.VMEM((devices, CAP, table.shape[1]), BF16),
            pltpu.VMEM((devices, CAP, table.shape[1]), BF16),
            pltpu.SemaphoreType.DMA,
            pltpu.SemaphoreType.DMA,
            pltpu.SemaphoreType.DMA((groups,)),
            pltpu.SemaphoreType.DMA((groups,)),
            pltpu.SemaphoreType.DMA,
            pltpu.SemaphoreType.DMA((groups,)),
        ],
        compiler_params=pltpu.CompilerParams(
            collective_id=0, has_side_effects=True, vmem_limit_bytes=48 << 20
        ),
        name="fetch",
    )(owner, slot, table)


def attend_kernel(
    index_ref, rows_ref, wq_ref, wk_ref, wv_ref, wg_ref, wo_ref, gain_ref, out_ref,
    embed, fq, fk, values, gates, intra, state, packed, from_each, earlier, entering,
    out_a, in_a, out_b, in_b,
):
    ctx_size = lax.axis_size("ctx")
    ctx, user = lax.axis_index("ctx"), lax.axis_index("user")
    barrier = pltpu.get_barrier_semaphore()

    def greet(k, carry):
        pl.semaphore_signal(
            barrier, inc=1, device_id=((ctx + k) % ctx_size, user), device_id_type=MESH
        )
        return carry

    lax.fori_loop(1, ctx_size, greet, 0)

    parts, positions = index_ref.shape
    chunks = positions // CHUNK

    def collect(b, carry):
        for i in range(16):
            for j in range(parts):
                embed[j, pl.ds(b * 16 + i, 1)] = rows_ref[pl.ds(index_ref[j, b * 16 + i], 1)]
        return carry

    lax.fori_loop(0, positions // 16, collect, 0)

    def feature(v):
        v = v.astype(BF16).astype(F32)
        return jnp.where(v > 0, v + 1.0, jnp.exp(jnp.minimum(v, 0.0))).astype(BF16)

    running = [jnp.zeros((HEAD, HEAD), F32)] * HEADS
    for c in range(chunks):
        at = pl.ds(c * CHUNK, CHUNK)
        e = jnp.concatenate([embed[j, at] for j in range(parts)], axis=1).astype(BF16)
        k = feature(jnp.dot(e, wk_ref[...], preferred_element_type=F32))
        v = jnp.dot(e, wv_ref[...], preferred_element_type=F32).astype(BF16)
        fk[at] = k
        values[at] = v
        for h in range(HEADS):
            s = slice(h * HEAD, (h + 1) * HEAD)
            state[c, h] = running[h]
            running[h] = running[h] + lax.dot_general(
                k[:, s], v[:, s], (((0,), (0,)), ((), ())), preferred_element_type=F32
            )
    rows = HEADS * HEAD // ctx_size
    for h in range(HEADS):
        for i in range(HEAD // rows):
            packed[h * (HEAD // rows) + i] = running[h][i * rows : (i + 1) * rows].astype(BF16)

    pl.semaphore_wait(barrier, ctx_size - 1)

    def part_out(k, carry):
        other = (ctx + k) % ctx_size
        pltpu.make_async_remote_copy(
            packed.at[other], from_each.at[ctx], out_a, in_a,
            device_id=(other, user), device_id_type=MESH,
        ).start()
        return carry

    lax.fori_loop(1, ctx_size, part_out, 0)
    from_each[ctx] = packed[ctx]

    causal = lax.broadcasted_iota(jnp.int32, (CHUNK, CHUNK), 0) >= lax.broadcasted_iota(
        jnp.int32, (CHUNK, CHUNK), 1
    )

    def local(c):
        at = pl.ds(c * CHUNK, CHUNK)
        e = jnp.concatenate([embed[j, at] for j in range(parts)], axis=1).astype(BF16)
        q = feature(jnp.dot(e, wq_ref[...], preferred_element_type=F32))
        fq[at] = q
        gates[at] = jnp.dot(e, wg_ref[...], preferred_element_type=F32).astype(BF16)
        for h in range(HEADS):
            s = slice(h * HEAD, (h + 1) * HEAD)
            scores = lax.dot_general(
                q[:, s], fk[at, s], (((1,), (1,)), ((), ())), preferred_element_type=F32
            )
            scores = jnp.where(causal, scores, 0.0).astype(BF16)
            intra[at, s] = jnp.dot(scores, values[at, s], preferred_element_type=F32)

    for c in range(chunks // 2):
        local(c)

    some = packed.at[pl.ds(0, ctx_size - 1)]
    pltpu.make_async_copy(some, some, in_a).wait()
    pltpu.make_async_copy(some, some, out_a).wait()
    sofar = jnp.zeros((rows, HEAD), F32)
    for i in range(ctx_size):
        earlier[i] = sofar.astype(BF16)
        sofar = sofar + from_each[i].astype(F32)

    def part_back(k, carry):
        other = (ctx + k) % ctx_size
        pltpu.make_async_remote_copy(
            earlier.at[other], entering.at[ctx], out_b, in_b,
            device_id=(other, user), device_id_type=MESH,
        ).start()
        return carry

    lax.fori_loop(1, ctx_size, part_back, 0)
    entering[ctx] = earlier[ctx]

    for c in range(chunks // 2, chunks):
        local(c)

    pltpu.make_async_copy(some, some, in_b).wait()
    pltpu.make_async_copy(some, some, out_b).wait()

    for c in range(chunks):
        at = pl.ds(c * CHUNK, CHUNK)
        heads = []
        for h in range(HEADS):
            s = slice(h * HEAD, (h + 1) * HEAD)
            n = HEAD // rows
            came = entering[h * n : (h + 1) * n].reshape(HEAD, HEAD).astype(F32)
            within = (state[c, h] + came).astype(BF16)
            mixed = intra[at, s] + jnp.dot(fq[at, s], within, preferred_element_type=F32)
            square = jnp.mean(mixed * mixed, axis=1, keepdims=True)
            gate = gates[at, s].astype(F32)
            normed = mixed * lax.rsqrt(square + 1e-6) * gain_ref[:, s]
            heads.append((normed * (gate / (1.0 + jnp.exp(-gate)))).astype(BF16))
        out_ref[at] = jnp.dot(
            jnp.concatenate(heads, axis=1), wo_ref[...], preferred_element_type=F32
        ).astype(BF16)


def attend(index, rows, wq, wk, wv, wg, wo, gain):
    ctx_size = lax.axis_size("ctx")
    parts, positions = index.shape
    width = wq.shape[1]
    vmem = pl.BlockSpec(memory_space=pltpu.VMEM)
    piece = pltpu.VMEM((ctx_size, HEADS * HEAD // ctx_size, HEAD), BF16)
    return pl.pallas_call(
        attend_kernel,
        out_shape=jax.ShapeDtypeStruct((positions, width), BF16),
        in_specs=[pl.BlockSpec(memory_space=pltpu.SMEM)] + [vmem] * 7,
        out_specs=vmem,
        scratch_shapes=[
            pltpu.VMEM((parts, positions, width // parts), F32),
            pltpu.VMEM((positions, width), BF16),
            pltpu.VMEM((positions, width), BF16),
            pltpu.VMEM((positions, width), BF16),
            pltpu.VMEM((positions, width), BF16),
            pltpu.VMEM((positions, width), F32),
            pltpu.VMEM((positions // CHUNK, HEADS, HEAD, HEAD), F32),
            piece, piece, piece, piece,
            pltpu.SemaphoreType.DMA,
            pltpu.SemaphoreType.DMA,
            pltpu.SemaphoreType.DMA,
            pltpu.SemaphoreType.DMA,
        ],
        compiler_params=pltpu.CompilerParams(
            collective_id=1, has_side_effects=True, vmem_limit_bytes=48 << 20
        ),
        name="attend",
    )(index, rows, wq, wk, wv, wg, wo, gain)


def shards(
    robe_array, block_owner, block_slot, w_query, w_key, w_value, w_gate, w_output, head_gain
):
    owner = jnp.swapaxes(block_owner[0], 0, 1)
    slot = jnp.swapaxes(block_slot[0], 0, 1)
    rows, index = fetch(owner, slot, robe_array)
    encoded = attend(
        index, rows.reshape(-1, rows.shape[2]), w_query, w_key, w_value, w_gate, w_output,
        head_gain.reshape(1, -1),
    )
    return encoded[None]


def solution(mesh):
    return jax.shard_map(
        shards,
        mesh=mesh,
        in_specs=(
            P(("ctx", "user"), None),
            P("user", "ctx", None),
            P("user", "ctx", None),
            P(),
            P(),
            P(),
            P(),
            P(),
            P(),
        ),
        out_specs=P("user", "ctx", None),
        check_vma=False,
    )
```

```python
import jax
import jax.numpy as jnp
from jax import lax
from jax.experimental import pallas as pl
from jax.experimental.pallas import tpu as pltpu
from jax.sharding import PartitionSpec as P

MESH = pl.DeviceIdType.MESH
HEADS = 4
HEAD = 128
CAP = 80
GROUP = 16
CHUNK = 256
F32 = jnp.float32
BF16 = jnp.bfloat16


def moved(k, sign):
    c, y = lax.axis_index("ctx"), lax.axis_index("user")
    core, r = k % 2, k // 2
    a, b, e = r % 4, (r // 4) % 4, r // 16
    z = (c // 8 + 8 + sign * (a + b + e)) % 4
    x = ((c // 2) % 4 + 8 + sign * a) % 4
    u = (y + 8 + sign * (a + b)) % 4
    return z * 8 + x * 2 + (c + core) % 2, u


def encoder_kernel(
    own_hbm, slot_hbm, table_hbm, wq_hbm, wk_hbm, wv_hbm, wg_hbm, wo_hbm, gain_hbm, out_ref,
    own_ref, slot_ref, packed, wq_ref, wk_ref, wv_ref, wg_ref, wo_ref, gain_ref,
    ranked, index_ref, req, landed, arrived, table, gathered, send, recv, rows_ref,
    embed, fq, fk, values, gates, intra, state, parcel, from_each, earlier, entering,
    loaded, index_in, req_out, req_in, read_in, row_out, row_in, out_a, in_a, out_b, in_b,
):
    devices = send.shape[0]
    groups = devices // GROUP
    users = lax.axis_size("user")
    me = lax.axis_index("ctx") * users + lax.axis_index("user")
    barrier = pltpu.get_barrier_semaphore()

    loads = [
        pltpu.make_async_copy(source, target, loaded.at[n])
        for n, (source, target) in enumerate(
            (
                (own_hbm, own_ref), (slot_hbm, slot_ref), (table_hbm, packed),
                (wk_hbm, wk_ref), (wv_hbm, wv_ref), (wq_hbm, wq_ref), (wg_hbm, wg_ref),
                (wo_hbm, wo_ref), (gain_hbm, gain_ref),
            )
        )
    ]
    for load in loads:
        load.start()
    loads[0].wait()
    loads[1].wait()

    parts, positions = own_ref.shape
    device_row = lax.broadcasted_iota(jnp.int32, (devices, CHUNK), 0)
    rank_row = lax.broadcasted_iota(jnp.int32, (128, CHUNK), 0)
    upper = jnp.where(
        lax.broadcasted_iota(jnp.int32, (CHUNK, CHUNK), 0)
        <= lax.broadcasted_iota(jnp.int32, (CHUNK, CHUNK), 1),
        1.0, 0.0,
    ).astype(BF16)
    before = jnp.zeros((devices, 1), F32)
    greeted, greetings = 0, devices * CHUNK // (parts * positions)
    total = jnp.zeros((devices, 256), F32)
    for j in range(parts):
        for p in range(0, positions, CHUNK):
            for k in range(greeted, greeted + greetings):
                if k > 0:
                    pl.semaphore_signal(
                        barrier, inc=1, device_id=moved(k, 1), device_id_type=MESH
                    )
            greeted += greetings
            own = own_ref[j : j + 1, p : p + CHUNK]
            slot = slot_ref[j : j + 1, p : p + CHUNK]
            named = device_row == own
            hot = jnp.where(named, 1.0, 0.0).astype(BF16)
            count = jnp.dot(hot, upper, preferred_element_type=F32) + before
            before = count[:, CHUNK - 1 :]
            rank = jnp.sum(jnp.where(named, count, 0.0), axis=0, keepdims=True).astype(jnp.int32) - 1
            spot = jnp.minimum(jnp.maximum(own * CAP + rank, 0), devices * CAP - 1)
            ranked[j : j + 1, p : p + CHUNK] = spot
            at_rank = rank_row == rank
            high = jnp.where(at_rank, (slot >> 6).astype(F32), 0.0).astype(BF16)
            low = jnp.where(at_rank, (slot & 63).astype(F32), 0.0).astype(BF16)
            total += lax.dot_general(
                hot, jnp.concatenate([high, low], axis=0), (((1,), (1,)), ((), ())),
                preferred_element_type=F32,
            )
    asked = (total[:, :128] * 64.0 + total[:, 128:]).astype(jnp.int32)
    req[...] = jnp.minimum(jnp.maximum(asked, 0), table.shape[0] - 1)
    landed[pl.ds(0, 1)] = req[pl.ds(me, 1)]
    place = pltpu.make_async_copy(ranked, index_ref, index_in)
    place.start()
    loads[2].wait()

    def widen(k, carry):
        s = pl.ds(pl.multiple_of(k * 256, 256), 256)
        table[s] = packed[s].astype(F32)
        return carry

    lax.fori_loop(0, table.shape[0] // 256, widen, 0)
    pl.semaphore_wait(barrier, devices - 1)

    def ask(k, carry):
        ctx, user = moved(k, 1)
        pltpu.make_async_remote_copy(
            req.at[pl.ds(ctx * users + user, 1)], landed.at[pl.ds(k, 1)], req_out,
            req_in.at[k // GROUP], device_id=(ctx, user), device_id_type=MESH,
        ).start()
        return carry

    def gather(k):
        for i in range(CAP):
            gathered[pl.ds(i, 1)] = table[pl.ds(arrived[k, i], 1)]
        return gathered[...].astype(BF16)

    def answer(k, carry):
        ctx, user = moved(k, -1)
        send[k] = gather(k)
        pltpu.make_async_remote_copy(
            send.at[k], recv.at[me], row_out, row_in.at[k // GROUP],
            device_id=(ctx, user), device_id_type=MESH,
        ).start()
        return carry

    def read(g):
        some = landed.at[pl.ds(g * GROUP, GROUP)]
        return pltpu.make_async_copy(some, arrived.at[pl.ds(g * GROUP, GROUP)], read_in.at[g])

    def come(g):
        some = req.at[pl.ds(0, GROUP - (1 if g == 0 else 0))]
        pltpu.make_async_copy(some, some, req_in.at[g]).wait()
        read(g).start()

    def asks(g):
        lax.fori_loop(g * GROUP + (1 if g == 0 else 0), (g + 1) * GROUP, ask, 0, unroll=True)

    for g in range(groups):
        asks(g)
    come(0)
    for g in range(groups):
        if g + 1 < groups:
            come(g + 1)
        read(g).wait()
        lax.fori_loop(g * GROUP + (1 if g == 0 else 0), (g + 1) * GROUP, answer, 0)
    recv[me] = gather(0)

    def unpack(k, carry):
        ctx, user = moved(k, 1)
        owner = ctx * users + user
        s = pl.ds(pl.multiple_of(owner * CAP, CAP), CAP)
        rows_ref[s] = recv[owner].astype(F32)
        return carry

    for g in range(groups):
        some = recv.at[pl.ds(0, GROUP - (1 if g == 0 else 0))]
        pltpu.make_async_copy(some, some, row_in.at[g]).wait()
        lax.fori_loop(g * GROUP, (g + 1) * GROUP, unpack, 0)
    ctx_size = lax.axis_size("ctx")
    ctx, user = lax.axis_index("ctx"), lax.axis_index("user")
    chunks = positions // CHUNK

    place.wait()

    def collect(b, carry):
        for i in range(16):
            for j in range(parts):
                embed[j, pl.ds(b * 16 + i, 1)] = rows_ref[pl.ds(index_ref[j, b * 16 + i], 1)]
        return carry

    lax.fori_loop(0, positions // 16, collect, 0)

    for load in loads[3:]:
        load.wait()

    def feature(v):
        v = v.astype(BF16).astype(F32)
        return jnp.where(v > 0, v + 1.0, jnp.exp(jnp.minimum(v, 0.0))).astype(BF16)

    running = [jnp.zeros((HEAD, HEAD), F32)] * HEADS
    for c in range(chunks):
        at = pl.ds(c * CHUNK, CHUNK)
        e = jnp.concatenate([embed[j, at] for j in range(parts)], axis=1).astype(BF16)
        k = feature(jnp.dot(e, wk_ref[...], preferred_element_type=F32))
        v = jnp.dot(e, wv_ref[...], preferred_element_type=F32).astype(BF16)
        fk[at] = k
        values[at] = v
        for h in range(HEADS):
            s = slice(h * HEAD, (h + 1) * HEAD)
            state[c, h] = running[h]
            running[h] = running[h] + lax.dot_general(
                k[:, s], v[:, s], (((0,), (0,)), ((), ())), preferred_element_type=F32
            )
    rows = HEADS * HEAD // ctx_size
    for h in range(HEADS):
        for i in range(HEAD // rows):
            parcel[h * (HEAD // rows) + i] = running[h][i * rows : (i + 1) * rows].astype(BF16)

    def part_out(k, carry):
        other = (ctx + k) % ctx_size
        pltpu.make_async_remote_copy(
            parcel.at[other], from_each.at[ctx], out_a, in_a,
            device_id=(other, user), device_id_type=MESH,
        ).start()
        return carry

    lax.fori_loop(1, ctx_size, part_out, 0)
    from_each[ctx] = parcel[ctx]

    causal = lax.broadcasted_iota(jnp.int32, (CHUNK, CHUNK), 0) >= lax.broadcasted_iota(
        jnp.int32, (CHUNK, CHUNK), 1
    )

    def local(c):
        at = pl.ds(c * CHUNK, CHUNK)
        e = jnp.concatenate([embed[j, at] for j in range(parts)], axis=1).astype(BF16)
        q = feature(jnp.dot(e, wq_ref[...], preferred_element_type=F32))
        fq[at] = q
        gates[at] = jnp.dot(e, wg_ref[...], preferred_element_type=F32).astype(BF16)
        for h in range(HEADS):
            s = slice(h * HEAD, (h + 1) * HEAD)
            scores = lax.dot_general(
                q[:, s], fk[at, s], (((1,), (1,)), ((), ())), preferred_element_type=F32
            )
            scores = jnp.where(causal, scores, 0.0).astype(BF16)
            intra[at, s] = jnp.dot(scores, values[at, s], preferred_element_type=F32)

    for c in range(chunks // 2):
        local(c)

    some = parcel.at[pl.ds(0, ctx_size - 1)]
    pltpu.make_async_copy(some, some, in_a).wait()
    pltpu.make_async_copy(some, some, out_a).wait()
    sofar = jnp.zeros((rows, HEAD), F32)
    for i in range(ctx_size):
        earlier[i] = sofar.astype(BF16)
        sofar = sofar + from_each[i].astype(F32)

    def part_back(k, carry):
        other = (ctx + k) % ctx_size
        pltpu.make_async_remote_copy(
            earlier.at[other], entering.at[ctx], out_b, in_b,
            device_id=(other, user), device_id_type=MESH,
        ).start()
        return carry

    lax.fori_loop(1, ctx_size, part_back, 0)
    entering[ctx] = earlier[ctx]

    for c in range(chunks // 2, chunks):
        local(c)

    pltpu.make_async_copy(some, some, in_b).wait()
    pltpu.make_async_copy(some, some, out_b).wait()

    for c in range(chunks):
        at = pl.ds(c * CHUNK, CHUNK)
        heads = []
        for h in range(HEADS):
            s = slice(h * HEAD, (h + 1) * HEAD)
            n = HEAD // rows
            came = entering[h * n : (h + 1) * n].reshape(HEAD, HEAD).astype(F32)
            within = (state[c, h] + came).astype(BF16)
            mixed = intra[at, s] + jnp.dot(fq[at, s], within, preferred_element_type=F32)
            square = jnp.mean(mixed * mixed, axis=1, keepdims=True)
            gate = gates[at, s].astype(F32)
            normed = mixed * lax.rsqrt(square + 1e-6) * gain_ref[:, s]
            heads.append((normed * (gate / (1.0 + jnp.exp(-gate)))).astype(BF16))
        out_ref[at] = jnp.dot(
            jnp.concatenate(heads, axis=1), wo_ref[...], preferred_element_type=F32
        ).astype(BF16)
    some = req.at[pl.ds(0, devices - 1)]
    pltpu.make_async_copy(some, some, req_out).wait()
    some = send.at[pl.ds(0, devices - 1)]
    pltpu.make_async_copy(some, some, row_out).wait()


def encoder(owner, slot, table, wq, wk, wv, wg, wo, gain):
    ctx_size = lax.axis_size("ctx")
    devices = ctx_size * lax.axis_size("user")
    groups = devices // GROUP
    parts, positions = owner.shape
    block = table.shape[1]
    width = wq.shape[1]
    args = (owner, slot, table, wq, wk, wv, wg, wo, gain)
    whole = pltpu.VMEM((positions, width), BF16)
    piece = pltpu.VMEM((ctx_size, HEADS * HEAD // ctx_size, HEAD), BF16)
    one, many = pltpu.SemaphoreType.DMA, pltpu.SemaphoreType.DMA((groups,))
    return pl.pallas_call(
        encoder_kernel,
        out_shape=jax.ShapeDtypeStruct((positions, width), BF16),
        in_specs=[pl.BlockSpec(memory_space=pltpu.HBM)] * len(args),
        out_specs=pl.BlockSpec(memory_space=pltpu.VMEM),
        scratch_shapes=[pltpu.VMEM(a.shape, a.dtype) for a in args]
        + [
            pltpu.VMEM((parts, positions), jnp.int32),
            pltpu.SMEM((parts, positions), jnp.int32),
            pltpu.VMEM((devices, 128), jnp.int32),
            pltpu.VMEM((devices, 128), jnp.int32),
            pltpu.SMEM((devices, 128), jnp.int32),
            pltpu.VMEM(table.shape, F32),
            pltpu.VMEM((CAP, block), F32),
            pltpu.VMEM((devices, CAP, block), BF16),
            pltpu.VMEM((devices, CAP, block), BF16),
            pltpu.VMEM((devices * CAP, block), F32),
            pltpu.VMEM((parts, positions, block), F32),
            whole, whole, whole, whole,
            pltpu.VMEM((positions, width), F32),
            pltpu.VMEM((positions // CHUNK, HEADS, HEAD, HEAD), F32),
            piece, piece, piece, piece,
            pltpu.SemaphoreType.DMA((len(args),)),
            one, one, many, many, one, many, one, one, one, one,
        ],
        compiler_params=pltpu.CompilerParams(
            collective_id=0, has_side_effects=True, vmem_limit_bytes=40 << 20
        ),
        name="encoder",
    )(*args)


def shards(
    robe_array, block_owner, block_slot, w_query, w_key, w_value, w_gate, w_output, head_gain
):
    owner = jnp.swapaxes(block_owner[0], 0, 1)
    slot = jnp.swapaxes(block_slot[0], 0, 1)
    encoded = encoder(
        owner, slot, robe_array, w_query, w_key, w_value, w_gate, w_output,
        head_gain.reshape(1, -1),
    )
    return encoded[None]


def solution(mesh):
    return jax.shard_map(
        shards,
        mesh=mesh,
        in_specs=(
            P(("ctx", "user"), None),
            P("user", "ctx", None),
            P("user", "ctx", None),
            P(),
            P(),
            P(),
            P(),
            P(),
            P(),
        ),
        out_specs=P("user", "ctx", None),
        check_vma=False,
    )
```

```python
import jax
import jax.numpy as jnp
from jax import lax
from jax.experimental import pallas as pl
from jax.experimental.pallas import tpu as pltpu
from jax.sharding import PartitionSpec as P

MESH = pl.DeviceIdType.MESH
HEADS = 4
HEAD = 128
CAP = 80
GROUP = 16
CHUNK = 256
F32 = jnp.float32
BF16 = jnp.bfloat16


def moved(k, sign):
    c, y = lax.axis_index("ctx"), lax.axis_index("user")
    core, r = k % 2, k // 2
    a, b, e = r % 4, (r // 4) % 4, r // 16
    z = (c // 8 + 8 + sign * (a + b + e)) % 4
    x = ((c // 2) % 4 + 8 + sign * a) % 4
    u = (y + 8 + sign * (a + b)) % 4
    return z * 8 + x * 2 + (c + core) % 2, u


def encoder_kernel(
    own_hbm, slot_hbm, table_hbm, wq_hbm, wk_hbm, wv_hbm, wg_hbm, gain_hbm, out_ref,
    own_ref, slot_ref, packed, wq_ref, wk_ref, wv_ref, wg_ref, gain_ref,
    ranked, index_ref, req, mid, landed, arrived, table, gathered, send, recv, rows_ref,
    embed, fq, fk, values, scale, intra, state, parcel, from_each, earlier, entering,
    loaded, index_in, req_out, mid_in, mid_out, land_in, read_in, row_out, row_in, out_a, in_a, out_b, in_b,
):
    devices = send.shape[0]
    groups = devices // GROUP
    users = lax.axis_size("user")
    me = lax.axis_index("ctx") * users + lax.axis_index("user")
    ctx, user = lax.axis_index("ctx"), lax.axis_index("user")
    chips, lane_size = req.shape[0], req.shape[1]
    chip, lane = ctx // 2, ctx % 2 * users + user
    same_lane = [(((chip + k) % chips) * 2 + ctx % 2, user) for k in range(chips)]
    lanes = [(lane + k) % lane_size for k in range(lane_size)]
    same_chip = [(chip * 2 + q // users, q % users) for q in lanes]
    barrier = pltpu.get_barrier_semaphore()
    for peer in same_lane[1:] + same_chip[1:]:
        pl.semaphore_signal(barrier, inc=1, device_id=peer, device_id_type=MESH)

    loads = [
        pltpu.make_async_copy(source, target, loaded.at[n])
        for n, (source, target) in enumerate(
            (
                (own_hbm, own_ref), (slot_hbm, slot_ref), (table_hbm, packed),
                (wk_hbm, wk_ref), (wv_hbm, wv_ref), (wq_hbm, wq_ref), (wg_hbm, wg_ref),
                (gain_hbm, gain_ref),
            )
        )
    ]
    for load in loads:
        load.start()
    loads[0].wait()
    loads[1].wait()

    parts, positions = own_ref.shape
    device_row = lax.broadcasted_iota(jnp.int32, (devices, CHUNK), 0)
    rank_row = lax.broadcasted_iota(jnp.int32, (128, CHUNK), 0)
    upper = jnp.where(
        lax.broadcasted_iota(jnp.int32, (CHUNK, CHUNK), 0)
        <= lax.broadcasted_iota(jnp.int32, (CHUNK, CHUNK), 1),
        1.0, 0.0,
    ).astype(BF16)
    before = jnp.zeros((devices, 1), F32)
    total = jnp.zeros((devices, 256), F32)
    for j in range(parts):
        for p in range(0, positions, CHUNK):
            own = own_ref[j : j + 1, p : p + CHUNK]
            slot = slot_ref[j : j + 1, p : p + CHUNK]
            named = device_row == own
            hot = jnp.where(named, 1.0, 0.0).astype(BF16)
            count = jnp.dot(hot, upper, preferred_element_type=F32) + before
            before = count[:, CHUNK - 1 :]
            rank = jnp.sum(jnp.where(named, count, 0.0), axis=0, keepdims=True).astype(jnp.int32) - 1
            spot = jnp.minimum(jnp.maximum(own * CAP + rank, 0), devices * CAP - 1)
            ranked[j : j + 1, p : p + CHUNK] = spot
            at_rank = rank_row == rank
            high = jnp.where(at_rank, (slot >> 6).astype(F32), 0.0).astype(BF16)
            low = jnp.where(at_rank, (slot & 63).astype(F32), 0.0).astype(BF16)
            total += lax.dot_general(
                hot, jnp.concatenate([high, low], axis=0), (((1,), (1,)), ((), ())),
                preferred_element_type=F32,
            )
    asked = (total[:, :128] * 64.0 + total[:, 128:]).astype(jnp.int32)
    asked = jnp.minimum(jnp.maximum(asked, 0), table.shape[0] - 1)
    req[...] = asked.reshape(req.shape)
    mid[chip] = req[chip]
    place = pltpu.make_async_copy(ranked, index_ref, index_in)
    place.start()
    loads[2].wait()

    pl.semaphore_wait(barrier, chips + lane_size - 2)
    for peer in same_lane[1:]:
        pltpu.make_async_remote_copy(
            req.at[peer[0] // 2], mid.at[chip], req_out, mid_in,
            device_id=peer, device_id_type=MESH,
        ).start()

    def widen(k, carry):
        s = pl.ds(pl.multiple_of(k * 256, 256), 256)
        table[s] = packed[s].astype(F32)
        return carry

    lax.fori_loop(0, table.shape[0] // 256, widen, 0)
    some = req.at[pl.ds(0, chips - 1)]
    pltpu.make_async_copy(some, some, mid_in).wait()
    for peer, q in zip(same_chip[1:], lanes[1:]):
        pltpu.make_async_remote_copy(
            mid.at[:, pl.ds(q, 1)], landed.at[:, pl.ds(lane, 1)], mid_out, land_in,
            device_id=peer, device_id_type=MESH,
        ).start()
    mine = pltpu.make_async_copy(
        mid.at[:, pl.ds(lane, 1)], landed.at[:, pl.ds(lane, 1)], read_in.at[0]
    )
    mine.start()
    mine.wait()
    some = mid.at[:, pl.ds(0, lane_size - 1)]
    pltpu.make_async_copy(some, some, land_in).wait()
    read = pltpu.make_async_copy(landed, arrived, read_in.at[1])
    read.start()
    read.wait()

    def gather(ctx, user):
        for i in range(CAP):
            slot = arrived[ctx // 2, ctx % 2 * users + user, i]
            gathered[pl.ds(i, 1)] = table[pl.ds(slot, 1)]
        return gathered[...].astype(BF16)

    def answer(k, carry):
        asker = moved(k, -1)
        send[k] = gather(*asker)
        pltpu.make_async_remote_copy(
            send.at[k], recv.at[me], row_out, row_in.at[k // GROUP],
            device_id=asker, device_id_type=MESH,
        ).start()
        return carry

    lax.fori_loop(1, devices, answer, 0)
    recv[me] = gather(ctx, user)

    def unpack(k, carry):
        ctx, user = moved(k, 1)
        owner = ctx * users + user
        s = pl.ds(pl.multiple_of(owner * CAP, CAP), CAP)
        rows_ref[s] = recv[owner].astype(F32)
        return carry

    for g in range(groups):
        some = recv.at[pl.ds(0, GROUP - (1 if g == 0 else 0))]
        pltpu.make_async_copy(some, some, row_in.at[g]).wait()
        lax.fori_loop(g * GROUP, (g + 1) * GROUP, unpack, 0)
    ctx_size = lax.axis_size("ctx")
    chunks = positions // CHUNK

    place.wait()

    def collect(b, carry):
        for i in range(16):
            for j in range(parts):
                embed[j, pl.ds(b * 16 + i, 1)] = rows_ref[pl.ds(index_ref[j, b * 16 + i], 1)]
        return carry

    lax.fori_loop(0, positions // 16, collect, 0)

    for load in loads[3:]:
        load.wait()

    def feature(v):
        v = v.astype(BF16).astype(F32)
        return jnp.where(v > 0, v + 1.0, jnp.exp(jnp.minimum(v, 0.0))).astype(BF16)

    running = [jnp.zeros((HEAD, HEAD), F32)] * HEADS
    for c in range(chunks):
        at = pl.ds(c * CHUNK, CHUNK)
        e = jnp.concatenate([embed[j, at] for j in range(parts)], axis=1).astype(BF16)
        k = feature(jnp.dot(e, wk_ref[...], preferred_element_type=F32))
        v = jnp.dot(e, wv_ref[...], preferred_element_type=F32).astype(BF16)
        fk[at] = k
        values[at] = v
        for h in range(HEADS):
            s = slice(h * HEAD, (h + 1) * HEAD)
            state[c, h] = running[h]
            running[h] = running[h] + lax.dot_general(
                k[:, s], v[:, s], (((0,), (0,)), ((), ())), preferred_element_type=F32
            )
    rows = HEADS * HEAD // ctx_size
    for h in range(HEADS):
        for i in range(HEAD // rows):
            parcel[h * (HEAD // rows) + i] = running[h][i * rows : (i + 1) * rows].astype(BF16)

    def part_out(k, carry):
        other = (ctx + k) % ctx_size
        pltpu.make_async_remote_copy(
            parcel.at[other], from_each.at[ctx], out_a, in_a,
            device_id=(other, user), device_id_type=MESH,
        ).start()
        return carry

    lax.fori_loop(1, ctx_size, part_out, 0, unroll=True)
    from_each[ctx] = parcel[ctx]

    causal = lax.broadcasted_iota(jnp.int32, (CHUNK, CHUNK), 0) >= lax.broadcasted_iota(
        jnp.int32, (CHUNK, CHUNK), 1
    )

    def local(c):
        at = pl.ds(c * CHUNK, CHUNK)
        e = jnp.concatenate([embed[j, at] for j in range(parts)], axis=1).astype(BF16)
        q = feature(jnp.dot(e, wq_ref[...], preferred_element_type=F32))
        fq[at] = q
        gate = jnp.dot(e, wg_ref[...], preferred_element_type=F32).astype(BF16).astype(F32)
        scale[at] = gain_ref[...] * (gate / (1.0 + jnp.exp(-gate)))
        for h in range(HEADS):
            s = slice(h * HEAD, (h + 1) * HEAD)
            scores = lax.dot_general(
                q[:, s], fk[at, s], (((1,), (1,)), ((), ())), preferred_element_type=F32
            )
            scores = jnp.where(causal, scores, 0.0).astype(BF16)
            intra[at, s] = jnp.dot(scores, values[at, s], preferred_element_type=F32)

    for c in range(chunks // 2):
        local(c)

    some = parcel.at[pl.ds(0, ctx_size - 1)]
    pltpu.make_async_copy(some, some, in_a).wait()
    pltpu.make_async_copy(some, some, out_a).wait()
    sofar = jnp.zeros((rows, HEAD), F32)
    for i in range(ctx_size):
        earlier[i] = sofar.astype(BF16)
        sofar = sofar + from_each[i].astype(F32)

    def part_back(k, carry):
        other = (ctx + k) % ctx_size
        pltpu.make_async_remote_copy(
            earlier.at[other], entering.at[ctx], out_b, in_b,
            device_id=(other, user), device_id_type=MESH,
        ).start()
        return carry

    lax.fori_loop(1, ctx_size, part_back, 0, unroll=True)
    entering[ctx] = earlier[ctx]

    for c in range(chunks // 2, chunks):
        local(c)

    pltpu.make_async_copy(some, some, in_b).wait()
    pltpu.make_async_copy(some, some, out_b).wait()

    mean = jnp.full((HEAD, HEAD), 1.0 / HEAD, BF16)
    for c in range(chunks):
        at = pl.ds(c * CHUNK, CHUNK)
        heads = []
        for h in range(HEADS):
            s = slice(h * HEAD, (h + 1) * HEAD)
            n = HEAD // rows
            came = entering[h * n : (h + 1) * n].reshape(HEAD, HEAD).astype(F32)
            within = (state[c, h] + came).astype(BF16)
            mixed = intra[at, s] + jnp.dot(fq[at, s], within, preferred_element_type=F32)
            square = jnp.dot((mixed * mixed).astype(BF16), mean, preferred_element_type=F32)
            heads.append((mixed * lax.rsqrt(square + 1e-6) * scale[at, s]).astype(BF16))
        out_ref[at] = jnp.concatenate(heads, axis=1)
    some = req.at[pl.ds(0, chips - 1)]
    pltpu.make_async_copy(some, some, req_out).wait()
    some = mid.at[:, pl.ds(0, lane_size - 1)]
    pltpu.make_async_copy(some, some, mid_out).wait()
    some = send.at[pl.ds(0, devices - 1)]
    pltpu.make_async_copy(some, some, row_out).wait()


def encoder(owner, slot, table, wq, wk, wv, wg, gain):
    ctx_size = lax.axis_size("ctx")
    devices = ctx_size * lax.axis_size("user")
    groups = devices // GROUP
    parts, positions = owner.shape
    block = table.shape[1]
    width = wq.shape[1]
    args = (owner, slot, table, wq, wk, wv, wg, gain)
    requests = pltpu.VMEM((devices // 8, 8, 128), jnp.int32)
    whole = pltpu.VMEM((positions, width), BF16)
    piece = pltpu.VMEM((ctx_size, HEADS * HEAD // ctx_size, HEAD), BF16)
    one, many = pltpu.SemaphoreType.DMA, pltpu.SemaphoreType.DMA((groups,))
    return pl.pallas_call(
        encoder_kernel,
        out_shape=jax.ShapeDtypeStruct((positions, width), BF16),
        in_specs=[pl.BlockSpec(memory_space=pltpu.HBM)] * len(args),
        out_specs=pl.BlockSpec(memory_space=pltpu.VMEM),
        scratch_shapes=[pltpu.VMEM(a.shape, a.dtype) for a in args]
        + [
            pltpu.VMEM((parts, positions), jnp.int32),
            pltpu.SMEM((parts, positions), jnp.int32),
            requests, requests, requests,
            pltpu.SMEM((devices // 8, 8, 128), jnp.int32),
            pltpu.VMEM(table.shape, F32),
            pltpu.VMEM((CAP, block), F32),
            pltpu.VMEM((devices, CAP, block), BF16),
            pltpu.VMEM((devices, CAP, block), BF16),
            pltpu.VMEM((devices * CAP, block), F32),
            pltpu.VMEM((parts, positions, block), F32),
            whole, whole, whole,
            pltpu.VMEM((positions, width), F32),
            pltpu.VMEM((positions, width), F32),
            pltpu.VMEM((positions // CHUNK, HEADS, HEAD, HEAD), F32),
            piece, piece, piece, piece,
            pltpu.SemaphoreType.DMA((len(args),)),
            one, one, one, one, one, pltpu.SemaphoreType.DMA((2,)), one, many, one, one, one, one,
        ],
        compiler_params=pltpu.CompilerParams(
            collective_id=0, has_side_effects=True, vmem_limit_bytes=56 << 20
        ),
        name="encoder",
    )(*args)


def shards(
    robe_array, block_owner, block_slot, w_query, w_key, w_value, w_gate, w_output, head_gain
):
    owner = jnp.swapaxes(block_owner[0], 0, 1)
    slot = jnp.swapaxes(block_slot[0], 0, 1)
    gated = encoder(
        owner, slot, robe_array, w_query, w_key, w_value, w_gate, head_gain.reshape(1, -1)
    )
    encoded = jnp.dot(gated, w_output, preferred_element_type=F32).astype(BF16)
    return encoded[None]


def solution(mesh):
    return jax.shard_map(
        shards,
        mesh=mesh,
        in_specs=(
            P(("ctx", "user"), None),
            P("user", "ctx", None),
            P("user", "ctx", None),
            P(),
            P(),
            P(),
            P(),
            P(),
            P(),
        ),
        out_specs=P("user", "ctx", None),
        check_vma=False,
    )
```

```python
import jax
import jax.numpy as jnp
from jax import lax
from jax.experimental import pallas as pl
from jax.experimental.pallas import tpu as pltpu
from jax.sharding import PartitionSpec as P

MESH = pl.DeviceIdType.MESH
HEADS = 4
HEAD = 128
CAP = 80
GROUP = 16
CHUNK = 256
F32 = jnp.float32
BF16 = jnp.bfloat16


def moved(k, sign):
    c, y = lax.axis_index("ctx"), lax.axis_index("user")
    core, r = k % 2, k // 2
    a, b, e = r % 4, (r // 4) % 4, r // 16
    z = (c // 8 + 8 + sign * (a + b + e)) % 4
    x = ((c // 2) % 4 + 8 + sign * a) % 4
    u = (y + 8 + sign * (a + b)) % 4
    return z * 8 + x * 2 + (c + core) % 2, u


def encoder_kernel(
    own_hbm, slot_hbm, table_hbm, wq_hbm, wk_hbm, wv_hbm, wg_hbm, gain_hbm, out_ref,
    own_ref, slot_ref, packed, wq_ref, wk_ref, wv_ref, wg_ref, gain_ref,
    ranked, index_ref, req, landed, arrived, table, gathered, send, recv, rows_ref,
    embed, fq, fk, values, scale, intra, state, parcel, from_each, earlier, entering,
    loaded, index_in, all_in, req_out, req_in, read_in, row_out, row_in, out_a, in_a, out_b, in_b,
):
    devices = send.shape[0]
    groups = devices // GROUP
    users = lax.axis_size("user")
    me = lax.axis_index("ctx") * users + lax.axis_index("user")
    ctx, user = lax.axis_index("ctx"), lax.axis_index("user")
    lane_size = users * 2
    chips = devices // lane_size
    chip, lane = ctx // 2, ctx % 2 * users + user
    same_lane = [(((chip + k) % chips) * 2 + ctx % 2, user) for k in range(chips)]
    lanes = [(lane + k) % lane_size for k in range(lane_size)]
    same_chip = [(chip * 2 + q // users, q % users) for q in lanes]
    barrier = pltpu.get_barrier_semaphore()
    for peer in same_lane[1:] + same_chip[1:]:
        pl.semaphore_signal(barrier, inc=1, device_id=peer, device_id_type=MESH)

    loads = [
        pltpu.make_async_copy(source, target, loaded.at[n])
        for n, (source, target) in enumerate(
            (
                (own_hbm, own_ref), (slot_hbm, slot_ref), (table_hbm, packed),
                (wk_hbm, wk_ref), (wv_hbm, wv_ref), (wq_hbm, wq_ref), (wg_hbm, wg_ref),
                (gain_hbm, gain_ref),
            )
        )
    ]
    for load in loads:
        load.start()
    loads[0].wait()
    loads[1].wait()

    parts, positions = own_ref.shape
    device_row = lax.broadcasted_iota(jnp.int32, (devices, CHUNK), 0)
    rank_row = lax.broadcasted_iota(jnp.int32, (128, CHUNK), 0)
    upper = jnp.where(
        lax.broadcasted_iota(jnp.int32, (CHUNK, CHUNK), 0)
        <= lax.broadcasted_iota(jnp.int32, (CHUNK, CHUNK), 1),
        1.0, 0.0,
    ).astype(BF16)
    before = jnp.zeros((devices, 1), F32)
    total = jnp.zeros((devices, 256), F32)
    for j in range(parts):
        for p in range(0, positions, CHUNK):
            if j == parts - 1 and p == 0:
                pl.semaphore_wait(barrier, chips + lane_size - 2)
                for peer in same_chip[1:]:
                    pl.semaphore_signal(all_in, inc=1, device_id=peer, device_id_type=MESH)
            own = own_ref[j : j + 1, p : p + CHUNK]
            slot = slot_ref[j : j + 1, p : p + CHUNK]
            named = device_row == own
            hot = jnp.where(named, 1.0, 0.0).astype(BF16)
            count = jnp.dot(hot, upper, preferred_element_type=F32) + before
            before = count[:, CHUNK - 1 :]
            rank = jnp.sum(jnp.where(named, count, 0.0), axis=0, keepdims=True).astype(jnp.int32) - 1
            spot = jnp.minimum(jnp.maximum(own * CAP + rank, 0), devices * CAP - 1)
            ranked[j : j + 1, p : p + CHUNK] = spot
            at_rank = rank_row == rank
            high = jnp.where(at_rank, (slot >> 6).astype(F32), 0.0).astype(BF16)
            low = jnp.where(at_rank, (slot & 63).astype(F32), 0.0).astype(BF16)
            total += lax.dot_general(
                hot, jnp.concatenate([high, low], axis=0), (((1,), (1,)), ((), ())),
                preferred_element_type=F32,
            )
    asked = (total[:, :128] * 64.0 + total[:, 128:]).astype(jnp.int32)
    req[...] = jnp.minimum(jnp.maximum(asked, 0), table.shape[0] - 1)
    landed[pl.ds(0, 1)] = req[pl.ds(me, 1)]
    place = pltpu.make_async_copy(ranked, index_ref, index_in)
    place.start()

    loads[2].wait()

    def widen(k, carry):
        s = pl.ds(pl.multiple_of(k * 256, 256), 256)
        table[s] = packed[s].astype(F32)
        return carry

    lax.fori_loop(0, table.shape[0] // 256, widen, 0)
    pl.semaphore_wait(all_in, lane_size - 1)

    def ask(k, carry):
        ctx, user = moved(k, 1)
        pltpu.make_async_remote_copy(
            req.at[pl.ds(ctx * users + user, 1)], landed.at[pl.ds(k, 1)], req_out,
            req_in.at[k // GROUP], device_id=(ctx, user), device_id_type=MESH,
        ).start()
        return carry

    lax.fori_loop(1, devices, ask, 0, unroll=True)

    def read(g):
        some = landed.at[pl.ds(g * GROUP, GROUP)]
        return pltpu.make_async_copy(some, arrived.at[pl.ds(g * GROUP, GROUP)], read_in.at[g])

    def come(g):
        some = req.at[pl.ds(0, GROUP - (1 if g == 0 else 0))]
        pltpu.make_async_copy(some, some, req_in.at[g]).wait()
        read(g).start()

    def gather(k):
        for i in range(CAP):
            gathered[pl.ds(i, 1)] = table[pl.ds(arrived[k, i], 1)]
        return gathered[...].astype(BF16)

    def answer(k, carry):
        send[k] = gather(k)
        pltpu.make_async_remote_copy(
            send.at[k], recv.at[me], row_out, row_in.at[k // GROUP],
            device_id=moved(k, -1), device_id_type=MESH,
        ).start()
        return carry

    come(0)
    for g in range(groups):
        if g + 1 < groups:
            come(g + 1)
        read(g).wait()
        lax.fori_loop(g * GROUP + (1 if g == 0 else 0), (g + 1) * GROUP, answer, 0)
    recv[me] = gather(0)

    def unpack(k, carry):
        ctx, user = moved(k, 1)
        owner = ctx * users + user
        s = pl.ds(pl.multiple_of(owner * CAP, CAP), CAP)
        rows_ref[s] = recv[owner].astype(F32)
        return carry

    for g in range(groups):
        some = recv.at[pl.ds(0, GROUP - (1 if g == 0 else 0))]
        pltpu.make_async_copy(some, some, row_in.at[g]).wait()
        lax.fori_loop(g * GROUP, (g + 1) * GROUP, unpack, 0)
    ctx_size = lax.axis_size("ctx")
    chunks = positions // CHUNK

    place.wait()

    def collect(b, carry):
        for i in range(16):
            for j in range(parts):
                embed[j, pl.ds(b * 16 + i, 1)] = rows_ref[pl.ds(index_ref[j, b * 16 + i], 1)]
        return carry

    lax.fori_loop(0, positions // 16, collect, 0)

    for load in loads[3:]:
        load.wait()

    def feature(v):
        v = v.astype(BF16).astype(F32)
        return jnp.where(v > 0, v + 1.0, jnp.exp(jnp.minimum(v, 0.0))).astype(BF16)

    running = [jnp.zeros((HEAD, HEAD), F32)] * HEADS
    for c in range(chunks):
        at = pl.ds(c * CHUNK, CHUNK)
        e = jnp.concatenate([embed[j, at] for j in range(parts)], axis=1).astype(BF16)
        k = feature(jnp.dot(e, wk_ref[...], preferred_element_type=F32))
        v = jnp.dot(e, wv_ref[...], preferred_element_type=F32).astype(BF16)
        fk[at] = k
        values[at] = v
        for h in range(HEADS):
            s = slice(h * HEAD, (h + 1) * HEAD)
            state[c, h] = running[h]
            running[h] = running[h] + lax.dot_general(
                k[:, s], v[:, s], (((0,), (0,)), ((), ())), preferred_element_type=F32
            )
    rows = HEADS * HEAD // ctx_size
    for h in range(HEADS):
        for i in range(HEAD // rows):
            parcel[h * (HEAD // rows) + i] = running[h][i * rows : (i + 1) * rows].astype(BF16)

    def part_out(k, carry):
        other = (ctx + k) % ctx_size
        pltpu.make_async_remote_copy(
            parcel.at[other], from_each.at[ctx], out_a, in_a,
            device_id=(other, user), device_id_type=MESH,
        ).start()
        return carry

    lax.fori_loop(1, ctx_size, part_out, 0, unroll=True)
    from_each[ctx] = parcel[ctx]

    causal = lax.broadcasted_iota(jnp.int32, (CHUNK, CHUNK), 0) >= lax.broadcasted_iota(
        jnp.int32, (CHUNK, CHUNK), 1
    )

    def local(c):
        at = pl.ds(c * CHUNK, CHUNK)
        e = jnp.concatenate([embed[j, at] for j in range(parts)], axis=1).astype(BF16)
        q = feature(jnp.dot(e, wq_ref[...], preferred_element_type=F32))
        fq[at] = q
        gate = jnp.dot(e, wg_ref[...], preferred_element_type=F32).astype(BF16).astype(F32)
        scale[at] = gain_ref[...] * (gate / (1.0 + jnp.exp(-gate)))
        for h in range(HEADS):
            s = slice(h * HEAD, (h + 1) * HEAD)
            scores = lax.dot_general(
                q[:, s], fk[at, s], (((1,), (1,)), ((), ())), preferred_element_type=F32
            )
            scores = jnp.where(causal, scores, 0.0).astype(BF16)
            intra[at, s] = jnp.dot(scores, values[at, s], preferred_element_type=F32)

    for c in range(chunks // 2):
        local(c)

    some = parcel.at[pl.ds(0, ctx_size - 1)]
    pltpu.make_async_copy(some, some, in_a).wait()
    pltpu.make_async_copy(some, some, out_a).wait()
    sofar = jnp.zeros((rows, HEAD), F32)
    for i in range(ctx_size):
        earlier[i] = sofar.astype(BF16)
        sofar = sofar + from_each[i].astype(F32)

    def part_back(k, carry):
        other = (ctx + k) % ctx_size
        pltpu.make_async_remote_copy(
            earlier.at[other], entering.at[ctx], out_b, in_b,
            device_id=(other, user), device_id_type=MESH,
        ).start()
        return carry

    lax.fori_loop(1, ctx_size, part_back, 0, unroll=True)
    entering[ctx] = earlier[ctx]

    for c in range(chunks // 2, chunks):
        local(c)

    pltpu.make_async_copy(some, some, in_b).wait()
    pltpu.make_async_copy(some, some, out_b).wait()

    mean = jnp.full((HEAD, HEAD), 1.0 / HEAD, BF16)
    for c in range(chunks):
        at = pl.ds(c * CHUNK, CHUNK)
        heads = []
        for h in range(HEADS):
            s = slice(h * HEAD, (h + 1) * HEAD)
            n = HEAD // rows
            came = entering[h * n : (h + 1) * n].reshape(HEAD, HEAD).astype(F32)
            within = (state[c, h] + came).astype(BF16)
            mixed = intra[at, s] + jnp.dot(fq[at, s], within, preferred_element_type=F32)
            square = jnp.dot((mixed * mixed).astype(BF16), mean, preferred_element_type=F32)
            heads.append((mixed * lax.rsqrt(square + 1e-6) * scale[at, s]).astype(BF16))
        out_ref[at] = jnp.concatenate(heads, axis=1)
    some = req.at[pl.ds(0, devices - 1)]
    pltpu.make_async_copy(some, some, req_out).wait()
    some = send.at[pl.ds(0, devices - 1)]
    pltpu.make_async_copy(some, some, row_out).wait()


def encoder(owner, slot, table, wq, wk, wv, wg, gain):
    ctx_size = lax.axis_size("ctx")
    devices = ctx_size * lax.axis_size("user")
    groups = devices // GROUP
    parts, positions = owner.shape
    block = table.shape[1]
    width = wq.shape[1]
    args = (owner, slot, table, wq, wk, wv, wg, gain)
    requests = pltpu.VMEM((devices, 128), jnp.int32)
    whole = pltpu.VMEM((positions, width), BF16)
    piece = pltpu.VMEM((ctx_size, HEADS * HEAD // ctx_size, HEAD), BF16)
    one, many = pltpu.SemaphoreType.DMA, pltpu.SemaphoreType.DMA((groups,))
    return pl.pallas_call(
        encoder_kernel,
        out_shape=jax.ShapeDtypeStruct((positions, width), BF16),
        in_specs=[pl.BlockSpec(memory_space=pltpu.HBM)] * len(args),
        out_specs=pl.BlockSpec(memory_space=pltpu.VMEM),
        scratch_shapes=[pltpu.VMEM(a.shape, a.dtype) for a in args]
        + [
            pltpu.VMEM((parts, positions), jnp.int32),
            pltpu.SMEM((parts, positions), jnp.int32),
            requests, requests,
            pltpu.SMEM((devices, 128), jnp.int32),
            pltpu.VMEM(table.shape, F32),
            pltpu.VMEM((CAP, block), F32),
            pltpu.VMEM((devices, CAP, block), BF16),
            pltpu.VMEM((devices, CAP, block), BF16),
            pltpu.VMEM((devices * CAP, block), F32),
            pltpu.VMEM((parts, positions, block), F32),
            whole, whole, whole,
            pltpu.VMEM((positions, width), F32),
            pltpu.VMEM((positions, width), F32),
            pltpu.VMEM((positions // CHUNK, HEADS, HEAD, HEAD), F32),
            piece, piece, piece, piece,
            pltpu.SemaphoreType.DMA((len(args),)),
            one, pltpu.SemaphoreType.REGULAR, one, many, many, one, many, one, one, one, one,
        ],
        compiler_params=pltpu.CompilerParams(
            collective_id=0, has_side_effects=True, vmem_limit_bytes=56 << 20
        ),
        name="encoder",
    )(*args)


def shards(
    robe_array, block_owner, block_slot, w_query, w_key, w_value, w_gate, w_output, head_gain
):
    owner = jnp.swapaxes(block_owner[0], 0, 1)
    slot = jnp.swapaxes(block_slot[0], 0, 1)
    gated = encoder(
        owner, slot, robe_array, w_query, w_key, w_value, w_gate, head_gain.reshape(1, -1)
    )
    encoded = jnp.dot(gated, w_output, preferred_element_type=F32).astype(BF16)
    return encoded[None]


def solution(mesh):
    return jax.shard_map(
        shards,
        mesh=mesh,
        in_specs=(
            P(("ctx", "user"), None),
            P("user", "ctx", None),
            P("user", "ctx", None),
            P(),
            P(),
            P(),
            P(),
            P(),
            P(),
        ),
        out_specs=P("user", "ctx", None),
        check_vma=False,
    )
```

```python
import jax
import jax.numpy as jnp
from jax import lax
from jax.experimental import pallas as pl
from jax.experimental.pallas import tpu as pltpu
from jax.sharding import PartitionSpec as P

MESH = pl.DeviceIdType.MESH
HEADS = 4
HEAD = 128
CAP = 80
GROUP = 16
CHUNK = 256
F32 = jnp.float32
BF16 = jnp.bfloat16


def moved(k, sign):
    c, y = lax.axis_index("ctx"), lax.axis_index("user")
    core, r = k % 2, k // 2
    a, b, e = r % 4, (r // 4) % 4, r // 16
    z = (c // 8 + 8 + sign * (a + b + e)) % 4
    x = ((c // 2) % 4 + 8 + sign * a) % 4
    u = (y + 8 + sign * (a + b)) % 4
    return z * 8 + x * 2 + (c + core) % 2, u


def encoder_kernel(
    own_hbm, slot_hbm, table_hbm, wq_hbm, wk_hbm, wv_hbm, wg_hbm, gain_hbm, out_ref,
    own_ref, slot_ref, packed, wq_ref, wk_ref, wv_ref, wg_ref, gain_ref,
    ranked, index_ref, req, landed, arrived, table, gathered, send, recv, rows_ref,
    embed, fq, fk, values, scale, intra, state, parcel, from_each, earlier, entering,
    loaded, index_in, all_in, req_out, req_in, read_in, row_out, row_in, out_a, in_a, out_b, in_b,
):
    devices = send.shape[0]
    groups = devices // GROUP
    users = lax.axis_size("user")
    me = lax.axis_index("ctx") * users + lax.axis_index("user")
    ctx, user = lax.axis_index("ctx"), lax.axis_index("user")
    lane_size = users * 2
    chips = devices // lane_size
    chip, lane = ctx // 2, ctx % 2 * users + user
    same_lane = [(((chip + k) % chips) * 2 + ctx % 2, user) for k in range(chips)]
    lanes = [(lane + k) % lane_size for k in range(lane_size)]
    same_chip = [(chip * 2 + q // users, q % users) for q in lanes]
    barrier = pltpu.get_barrier_semaphore()
    for peer in same_lane[1:] + same_chip[1:]:
        pl.semaphore_signal(barrier, inc=1, device_id=peer, device_id_type=MESH)

    loads = [
        pltpu.make_async_copy(source, target, loaded.at[n])
        for n, (source, target) in enumerate(
            (
                (own_hbm, own_ref), (slot_hbm, slot_ref), (table_hbm, packed),
                (wk_hbm, wk_ref), (wv_hbm, wv_ref), (wq_hbm, wq_ref), (wg_hbm, wg_ref),
                (gain_hbm, gain_ref),
            )
        )
    ]
    for load in loads:
        load.start()
    loads[0].wait()
    loads[1].wait()

    parts, positions = own_ref.shape
    device_row = lax.broadcasted_iota(jnp.int32, (devices, CHUNK), 0)
    rank_row = lax.broadcasted_iota(jnp.int32, (128, CHUNK), 0)
    upper = jnp.where(
        lax.broadcasted_iota(jnp.int32, (CHUNK, CHUNK), 0)
        <= lax.broadcasted_iota(jnp.int32, (CHUNK, CHUNK), 1),
        1.0, 0.0,
    ).astype(BF16)
    before = jnp.zeros((devices, 1), F32)
    total = jnp.zeros((devices, 256), F32)
    for j in range(parts):
        for p in range(0, positions, CHUNK):
            if j == parts - 1 and p == 0:
                pl.semaphore_wait(barrier, chips + lane_size - 2)
                for peer in same_chip[1:]:
                    pl.semaphore_signal(all_in, inc=1, device_id=peer, device_id_type=MESH)
            own = own_ref[j : j + 1, p : p + CHUNK]
            slot = slot_ref[j : j + 1, p : p + CHUNK]
            named = device_row == own
            hot = jnp.where(named, 1.0, 0.0).astype(BF16)
            count = jnp.dot(hot, upper, preferred_element_type=F32) + before
            before = count[:, CHUNK - 1 :]
            rank = jnp.sum(jnp.where(named, count, 0.0), axis=0, keepdims=True).astype(jnp.int32) - 1
            spot = jnp.minimum(jnp.maximum(own * CAP + rank, 0), devices * CAP - 1)
            for b in range(CHUNK // 128):
                row = (j * positions + p) // 128 + b
                ranked[row : row + 1] = spot[:, b * 128 : (b + 1) * 128]
            at_rank = rank_row == rank
            high = jnp.where(at_rank, (slot >> 6).astype(F32), 0.0).astype(BF16)
            low = jnp.where(at_rank, (slot & 63).astype(F32), 0.0).astype(BF16)
            total += lax.dot_general(
                hot, jnp.concatenate([high, low], axis=0), (((1,), (1,)), ((), ())),
                preferred_element_type=F32,
            )
    asked = (total[:, :128] * 64.0 + total[:, 128:]).astype(jnp.int32)
    req[...] = jnp.minimum(jnp.maximum(asked, 0), table.shape[0] - 1)
    landed[pl.ds(0, 1)] = req[pl.ds(me, 1)]
    place = pltpu.make_async_copy(ranked, index_ref, index_in)
    place.start()

    loads[2].wait()

    def widen(k, carry):
        s = pl.ds(pl.multiple_of(k * 256, 256), 256)
        table[s] = packed[s].astype(F32)
        return carry

    lax.fori_loop(0, table.shape[0] // 256, widen, 0)
    pl.semaphore_wait(all_in, lane_size - 1)

    def ask(k, carry):
        ctx, user = moved(k, 1)
        pltpu.make_async_remote_copy(
            req.at[pl.ds(ctx * users + user, 1)], landed.at[pl.ds(k, 1)], req_out,
            req_in.at[k // GROUP], device_id=(ctx, user), device_id_type=MESH,
        ).start()
        return carry

    lax.fori_loop(1, devices, ask, 0, unroll=True)

    def read(g):
        some = landed.at[pl.ds(g * GROUP, GROUP)]
        return pltpu.make_async_copy(some, arrived.at[pl.ds(g * GROUP, GROUP)], read_in.at[g])

    def come(g):
        some = req.at[pl.ds(0, GROUP - (1 if g == 0 else 0))]
        pltpu.make_async_copy(some, some, req_in.at[g]).wait()
        read(g).start()

    def gather(k):
        for i in range(CAP):
            gathered[pl.ds(i, 1)] = table[pl.ds(arrived[k, i], 1)]
        return gathered[...].astype(BF16)

    def answer(k, carry):
        send[k] = gather(k)
        pltpu.make_async_remote_copy(
            send.at[k], recv.at[me], row_out, row_in.at[k // GROUP],
            device_id=moved(k, -1), device_id_type=MESH,
        ).start()
        return carry

    come(0)
    for g in range(groups):
        if g + 1 < groups:
            come(g + 1)
        read(g).wait()
        lax.fori_loop(g * GROUP + (1 if g == 0 else 0), (g + 1) * GROUP, answer, 0)
    recv[me] = gather(0)

    def unpack(k, carry):
        ctx, user = moved(k, 1)
        owner = ctx * users + user
        s = pl.ds(pl.multiple_of(owner * CAP, CAP), CAP)
        rows_ref[s] = recv[owner].astype(F32)
        return carry

    for g in range(groups):
        some = recv.at[pl.ds(0, GROUP - (1 if g == 0 else 0))]
        pltpu.make_async_copy(some, some, row_in.at[g]).wait()
        lax.fori_loop(g * GROUP, (g + 1) * GROUP, unpack, 0)
    ctx_size = lax.axis_size("ctx")
    chunks = positions // CHUNK

    place.wait()

    blocks = positions // 128

    def collect(b, carry):
        for i in range(128):
            for j in range(parts):
                row = rows_ref[pl.ds(index_ref[j * blocks + b, i], 1)]
                embed[j, pl.ds(b * 128 + i, 1)] = row
        return carry

    lax.fori_loop(0, blocks, collect, 0)

    for load in loads[3:]:
        load.wait()

    def feature(v):
        v = v.astype(BF16).astype(F32)
        return jnp.where(v > 0, v + 1.0, jnp.exp(jnp.minimum(v, 0.0))).astype(BF16)

    running = [jnp.zeros((HEAD, HEAD), F32)] * HEADS
    for c in range(chunks):
        at = pl.ds(c * CHUNK, CHUNK)
        e = jnp.concatenate([embed[j, at] for j in range(parts)], axis=1).astype(BF16)
        k = feature(jnp.dot(e, wk_ref[...], preferred_element_type=F32))
        v = jnp.dot(e, wv_ref[...], preferred_element_type=F32).astype(BF16)
        fk[at] = k
        values[at] = v
        for h in range(HEADS):
            s = slice(h * HEAD, (h + 1) * HEAD)
            state[c, h] = running[h]
            running[h] = running[h] + lax.dot_general(
                k[:, s], v[:, s], (((0,), (0,)), ((), ())), preferred_element_type=F32
            )
    rows = HEADS * HEAD // ctx_size
    for h in range(HEADS):
        for i in range(HEAD // rows):
            parcel[h * (HEAD // rows) + i] = running[h][i * rows : (i + 1) * rows].astype(BF16)

    ways = [(dz, dx, dc) for dz in range(4) for dx in range(4) for dc in range(2)]
    ways.sort(key=lambda w: -(min(w[0], 4 - w[0]) + min(w[1], 4 - w[1]) + 0.1 * w[2]))
    others = [
        (ctx // 8 + dz) % 4 * 8 + (ctx // 2 + dx) % 4 * 2 + (ctx + dc) % 2
        for dz, dx, dc in ways[:-1]
    ]
    for other in others:
        pltpu.make_async_remote_copy(
            parcel.at[other], from_each.at[ctx], out_a, in_a,
            device_id=(other, user), device_id_type=MESH,
        ).start()
    from_each[ctx] = parcel[ctx]

    causal = lax.broadcasted_iota(jnp.int32, (CHUNK, CHUNK), 0) >= lax.broadcasted_iota(
        jnp.int32, (CHUNK, CHUNK), 1
    )

    def local(c):
        at = pl.ds(c * CHUNK, CHUNK)
        e = jnp.concatenate([embed[j, at] for j in range(parts)], axis=1).astype(BF16)
        q = feature(jnp.dot(e, wq_ref[...], preferred_element_type=F32))
        fq[at] = q
        gate = jnp.dot(e, wg_ref[...], preferred_element_type=F32).astype(BF16).astype(F32)
        scale[at] = gain_ref[...] * (gate / (1.0 + jnp.exp(-gate)))
        for h in range(HEADS):
            s = slice(h * HEAD, (h + 1) * HEAD)
            scores = lax.dot_general(
                q[:, s], fk[at, s], (((1,), (1,)), ((), ())), preferred_element_type=F32
            )
            scores = jnp.where(causal, scores, 0.0).astype(BF16)
            intra[at, s] = jnp.dot(scores, values[at, s], preferred_element_type=F32)

    for c in range(chunks // 2):
        local(c)

    some = parcel.at[pl.ds(0, ctx_size - 1)]
    pltpu.make_async_copy(some, some, in_a).wait()
    pltpu.make_async_copy(some, some, out_a).wait()
    sofar = jnp.zeros((rows, HEAD), F32)
    for i in range(ctx_size):
        earlier[i] = sofar.astype(BF16)
        sofar = sofar + from_each[i].astype(F32)

    for other in others:
        pltpu.make_async_remote_copy(
            earlier.at[other], entering.at[ctx], out_b, in_b,
            device_id=(other, user), device_id_type=MESH,
        ).start()
    entering[ctx] = earlier[ctx]

    for c in range(chunks // 2, chunks):
        local(c)

    pltpu.make_async_copy(some, some, in_b).wait()
    pltpu.make_async_copy(some, some, out_b).wait()

    mean = jnp.full((HEAD, HEAD), 1.0 / HEAD, BF16)
    for c in range(chunks):
        at = pl.ds(c * CHUNK, CHUNK)
        heads = []
        for h in range(HEADS):
            s = slice(h * HEAD, (h + 1) * HEAD)
            n = HEAD // rows
            came = entering[h * n : (h + 1) * n].reshape(HEAD, HEAD).astype(F32)
            within = (state[c, h] + came).astype(BF16)
            mixed = intra[at, s] + jnp.dot(fq[at, s], within, preferred_element_type=F32)
            square = jnp.dot((mixed * mixed).astype(BF16), mean, preferred_element_type=F32)
            heads.append((mixed * lax.rsqrt(square + 1e-6) * scale[at, s]).astype(BF16))
        out_ref[at] = jnp.concatenate(heads, axis=1)
    some = req.at[pl.ds(0, devices - 1)]
    pltpu.make_async_copy(some, some, req_out).wait()
    some = send.at[pl.ds(0, devices - 1)]
    pltpu.make_async_copy(some, some, row_out).wait()


def encoder(owner, slot, table, wq, wk, wv, wg, gain):
    ctx_size = lax.axis_size("ctx")
    devices = ctx_size * lax.axis_size("user")
    groups = devices // GROUP
    parts, positions = owner.shape
    block = table.shape[1]
    width = wq.shape[1]
    args = (owner, slot, table, wq, wk, wv, wg, gain)
    requests = pltpu.VMEM((devices, 128), jnp.int32)
    whole = pltpu.VMEM((positions, width), BF16)
    piece = pltpu.VMEM((ctx_size, HEADS * HEAD // ctx_size, HEAD), BF16)
    one, many = pltpu.SemaphoreType.DMA, pltpu.SemaphoreType.DMA((groups,))
    return pl.pallas_call(
        encoder_kernel,
        out_shape=jax.ShapeDtypeStruct((positions, width), BF16),
        in_specs=[pl.BlockSpec(memory_space=pltpu.HBM)] * len(args),
        out_specs=pl.BlockSpec(memory_space=pltpu.VMEM),
        scratch_shapes=[pltpu.VMEM(a.shape, a.dtype) for a in args]
        + [
            pltpu.VMEM((parts * positions // 128, 128), jnp.int32),
            pltpu.SMEM((parts * positions // 128, 128), jnp.int32),
            requests, requests,
            pltpu.SMEM((devices, 128), jnp.int32),
            pltpu.VMEM(table.shape, F32),
            pltpu.VMEM((CAP, block), F32),
            pltpu.VMEM((devices, CAP, block), BF16),
            pltpu.VMEM((devices, CAP, block), BF16),
            pltpu.VMEM((devices * CAP, block), F32),
            pltpu.VMEM((parts, positions, block), F32),
            whole, whole, whole,
            pltpu.VMEM((positions, width), F32),
            pltpu.VMEM((positions, width), F32),
            pltpu.VMEM((positions // CHUNK, HEADS, HEAD, HEAD), F32),
            piece, piece, piece, piece,
            pltpu.SemaphoreType.DMA((len(args),)),
            one, pltpu.SemaphoreType.REGULAR, one, many, many, one, many, one, one, one, one,
        ],
        compiler_params=pltpu.CompilerParams(
            collective_id=0, has_side_effects=True, vmem_limit_bytes=56 << 20
        ),
        name="encoder",
    )(*args)


def shards(
    robe_array, block_owner, block_slot, w_query, w_key, w_value, w_gate, w_output, head_gain
):
    owner = jnp.swapaxes(block_owner[0], 0, 1)
    slot = jnp.swapaxes(block_slot[0], 0, 1)
    gated = encoder(
        owner, slot, robe_array, w_query, w_key, w_value, w_gate, head_gain.reshape(1, -1)
    )
    encoded = jnp.dot(gated, w_output, preferred_element_type=F32).astype(BF16)
    return encoded[None]


def solution(mesh):
    return jax.shard_map(
        shards,
        mesh=mesh,
        in_specs=(
            P(("ctx", "user"), None),
            P("user", "ctx", None),
            P("user", "ctx", None),
            P(),
            P(),
            P(),
            P(),
            P(),
            P(),
        ),
        out_specs=P("user", "ctx", None),
        check_vma=False,
    )
```

```python
import jax
import jax.numpy as jnp
from jax import lax
from jax.experimental import pallas as pl
from jax.experimental.pallas import tpu as pltpu
from jax.sharding import PartitionSpec as P

MESH = pl.DeviceIdType.MESH
HEADS = 4
HEAD = 128
CAP = 80
GROUP = 16
CHUNK = 256
WIDE = 512
F32 = jnp.float32
BF16 = jnp.bfloat16


def moved(k, sign):
    c, y = lax.axis_index("ctx"), lax.axis_index("user")
    core, r = k % 2, k // 2
    a, b, e = r % 4, (r // 4) % 4, r // 16
    z = (c // 8 + 8 + sign * (a + b + e)) % 4
    x = ((c // 2) % 4 + 8 + sign * a) % 4
    u = (y + 8 + sign * (a + b)) % 4
    return z * 8 + x * 2 + (c + core) % 2, u


def encoder_kernel(
    own_hbm, slot_hbm, table_hbm, wq_hbm, wk_hbm, wv_hbm, wg_hbm, gain_hbm, out_hbm,
    own_ref, slot_ref, packed, wq_ref, wk_ref, wv_ref, wg_ref, gain_ref,
    ranked, index_ref, req, landed, arrived, table, gathered, send, recv, rows_ref,
    embed, items, gated, fq, fk, values, scale, intra, state, parcel, from_each, earlier, entering,
    loaded, stored, index_in, all_in, req_out, req_in, read_in, row_out, row_in, out_a, in_a, out_b, in_b,
):
    devices = send.shape[0]
    groups = devices // GROUP
    users = lax.axis_size("user")
    me = lax.axis_index("ctx") * users + lax.axis_index("user")
    ctx, user = lax.axis_index("ctx"), lax.axis_index("user")
    lane_size = users * 2
    chips = devices // lane_size
    chip, lane = ctx // 2, ctx % 2 * users + user
    same_lane = [(((chip + k) % chips) * 2 + ctx % 2, user) for k in range(chips)]
    lanes = [(lane + k) % lane_size for k in range(lane_size)]
    same_chip = [(chip * 2 + q // users, q % users) for q in lanes]
    barrier = pltpu.get_barrier_semaphore()
    for peer in same_lane[1:] + same_chip[1:]:
        pl.semaphore_signal(barrier, inc=1, device_id=peer, device_id_type=MESH)

    loads = [
        pltpu.make_async_copy(source, target, loaded.at[n])
        for n, (source, target) in enumerate(
            (
                (own_hbm, own_ref), (slot_hbm, slot_ref), (table_hbm, packed),
                (wk_hbm, wk_ref), (wv_hbm, wv_ref), (wq_hbm, wq_ref), (wg_hbm, wg_ref),
                (gain_hbm, gain_ref),
            )
        )
    ]
    for load in loads:
        load.start()
    loads[0].wait()
    loads[1].wait()

    parts, positions = own_ref.shape
    device_row = lax.broadcasted_iota(jnp.int32, (devices, CHUNK), 0)
    rank_row = lax.broadcasted_iota(jnp.int32, (128, CHUNK), 0)
    upper = jnp.where(
        lax.broadcasted_iota(jnp.int32, (CHUNK, CHUNK), 0)
        <= lax.broadcasted_iota(jnp.int32, (CHUNK, CHUNK), 1),
        1.0, 0.0,
    ).astype(BF16)
    before = jnp.zeros((devices, 1), F32)
    total = jnp.zeros((devices, 256), F32)
    for j in range(parts):
        for p in range(0, positions, CHUNK):
            if j == parts - 1 and p == 0:
                pl.semaphore_wait(barrier, chips + lane_size - 2)
                for peer in same_chip[1:]:
                    pl.semaphore_signal(all_in, inc=1, device_id=peer, device_id_type=MESH)
            own = own_ref[j : j + 1, p : p + CHUNK]
            slot = slot_ref[j : j + 1, p : p + CHUNK]
            named = device_row == own
            hot = jnp.where(named, 1.0, 0.0).astype(BF16)
            count = jnp.dot(hot, upper, preferred_element_type=F32) + before
            before = count[:, CHUNK - 1 :]
            rank = jnp.sum(jnp.where(named, count, 0.0), axis=0, keepdims=True).astype(jnp.int32) - 1
            spot = jnp.minimum(jnp.maximum(own * CAP + rank, 0), devices * CAP - 1)
            for b in range(CHUNK // 128):
                row = (j * positions + p) // 128 + b
                ranked[row : row + 1] = spot[:, b * 128 : (b + 1) * 128]
            at_rank = rank_row == rank
            high = jnp.where(at_rank, (slot >> 6).astype(F32), 0.0).astype(BF16)
            low = jnp.where(at_rank, (slot & 63).astype(F32), 0.0).astype(BF16)
            total += lax.dot_general(
                hot, jnp.concatenate([high, low], axis=0), (((1,), (1,)), ((), ())),
                preferred_element_type=F32,
            )
    asked = (total[:, :128] * 64.0 + total[:, 128:]).astype(jnp.int32)
    req[...] = jnp.minimum(jnp.maximum(asked, 0), table.shape[0] - 1)
    landed[pl.ds(0, 1)] = req[pl.ds(me, 1)]
    place = pltpu.make_async_copy(ranked, index_ref, index_in)
    place.start()

    loads[2].wait()

    def widen(k, carry):
        s = pl.ds(pl.multiple_of(k * 256, 256), 256)
        table[s] = packed[s].astype(F32)
        return carry

    lax.fori_loop(0, table.shape[0] // 256, widen, 0)
    pl.semaphore_wait(all_in, lane_size - 1)

    def ask(k, carry):
        ctx, user = moved(k, 1)
        pltpu.make_async_remote_copy(
            req.at[pl.ds(ctx * users + user, 1)], landed.at[pl.ds(k, 1)], req_out,
            req_in.at[k // GROUP], device_id=(ctx, user), device_id_type=MESH,
        ).start()
        return carry

    lax.fori_loop(1, devices, ask, 0, unroll=True)

    def read(g):
        some = landed.at[pl.ds(g * GROUP, GROUP)]
        return pltpu.make_async_copy(some, arrived.at[pl.ds(g * GROUP, GROUP)], read_in.at[g])

    def come(g):
        some = req.at[pl.ds(0, GROUP - (1 if g == 0 else 0))]
        pltpu.make_async_copy(some, some, req_in.at[g]).wait()
        read(g).start()

    def gather(k):
        for i in range(CAP):
            gathered[pl.ds(i, 1)] = table[pl.ds(arrived[k, i], 1)]
        return gathered[...].astype(BF16)

    def answer(k, carry):
        send[k] = gather(k)
        pltpu.make_async_remote_copy(
            send.at[k], recv.at[me], row_out, row_in.at[k // GROUP],
            device_id=moved(k, -1), device_id_type=MESH,
        ).start()
        return carry

    come(0)
    for g in range(groups):
        if g + 1 < groups:
            come(g + 1)
        read(g).wait()
        lax.fori_loop(g * GROUP + (1 if g == 0 else 0), (g + 1) * GROUP, answer, 0)
    recv[me] = gather(0)

    def unpack(k, carry):
        ctx, user = moved(k, 1)
        owner = ctx * users + user
        s = pl.ds(pl.multiple_of(owner * CAP, CAP), CAP)
        rows_ref[s] = recv[owner].astype(F32)
        return carry

    for g in range(groups):
        some = recv.at[pl.ds(0, GROUP - (1 if g == 0 else 0))]
        pltpu.make_async_copy(some, some, row_in.at[g]).wait()
        lax.fori_loop(g * GROUP, (g + 1) * GROUP, unpack, 0)
    ctx_size = lax.axis_size("ctx")
    chunks = positions // CHUNK

    place.wait()

    blocks = positions // 128

    def collect(b, carry):
        for i in range(128):
            for j in range(parts):
                row = rows_ref[pl.ds(index_ref[j * blocks + b, i], 1)]
                embed[j, pl.ds(b * 128 + i, 1)] = row
        return carry

    lax.fori_loop(0, blocks, collect, 0)

    for load in loads[3:]:
        load.wait()

    def feature(v):
        v = v.astype(BF16).astype(F32)
        return jnp.where(v > 0, v + 1.0, jnp.exp(jnp.minimum(v, 0.0))).astype(BF16)

    running = [jnp.zeros((HEAD, HEAD), F32)] * HEADS
    for w in range(positions // WIDE):
        at = pl.ds(w * WIDE, WIDE)
        e = jnp.concatenate([embed[j, at] for j in range(parts)], axis=1).astype(BF16)
        items[at] = e
        k = feature(jnp.dot(e, wk_ref[...], preferred_element_type=F32))
        v = jnp.dot(e, wv_ref[...], preferred_element_type=F32).astype(BF16)
        fk[at] = k
        values[at] = v
        for n in range(WIDE // CHUNK):
            r = slice(n * CHUNK, (n + 1) * CHUNK)
            for h in range(HEADS):
                s = slice(h * HEAD, (h + 1) * HEAD)
                state[w * (WIDE // CHUNK) + n, h] = running[h]
                running[h] = running[h] + lax.dot_general(
                    k[r, s], v[r, s], (((0,), (0,)), ((), ())), preferred_element_type=F32
                )
    rows = HEADS * HEAD // ctx_size
    for h in range(HEADS):
        for i in range(HEAD // rows):
            parcel[h * (HEAD // rows) + i] = running[h][i * rows : (i + 1) * rows].astype(BF16)

    ways = [(dz, dx, dc) for dz in range(4) for dx in range(4) for dc in range(2)]
    ways.sort(key=lambda w: -(min(w[0], 4 - w[0]) + min(w[1], 4 - w[1]) + 0.1 * w[2]))
    others = [
        (ctx // 8 + dz) % 4 * 8 + (ctx // 2 + dx) % 4 * 2 + (ctx + dc) % 2
        for dz, dx, dc in ways[:-1]
    ]
    for other in others:
        pltpu.make_async_remote_copy(
            parcel.at[other], from_each.at[ctx], out_a, in_a,
            device_id=(other, user), device_id_type=MESH,
        ).start()
    from_each[ctx] = parcel[ctx]

    causal = lax.broadcasted_iota(jnp.int32, (CHUNK, CHUNK), 0) >= lax.broadcasted_iota(
        jnp.int32, (CHUNK, CHUNK), 1
    )

    def local(w):
        whole = pl.ds(w * WIDE, WIDE)
        e = items[whole]
        q = feature(jnp.dot(e, wq_ref[...], preferred_element_type=F32))
        fq[whole] = q
        gate = jnp.dot(e, wg_ref[...], preferred_element_type=F32).astype(BF16).astype(F32)
        scale[whole] = gain_ref[...] * (gate / (1.0 + jnp.exp(-gate)))
        for n in range(WIDE // CHUNK):
            at = pl.ds(w * WIDE + n * CHUNK, CHUNK)
            for h in range(HEADS):
                s = slice(h * HEAD, (h + 1) * HEAD)
                scores = lax.dot_general(
                    q[n * CHUNK : (n + 1) * CHUNK, s], fk[at, s], (((1,), (1,)), ((), ())),
                    preferred_element_type=F32,
                )
                scores = jnp.where(causal, scores, 0.0).astype(BF16)
                intra[at, s] = jnp.dot(scores, values[at, s], preferred_element_type=F32)

    for w in range(positions // WIDE // 2):
        local(w)

    some = parcel.at[pl.ds(0, ctx_size - 1)]
    pltpu.make_async_copy(some, some, in_a).wait()
    pltpu.make_async_copy(some, some, out_a).wait()
    sofar = jnp.zeros((rows, HEAD), F32)
    for i in range(ctx_size):
        earlier[i] = sofar.astype(BF16)
        sofar = sofar + from_each[i].astype(F32)

    for other in others:
        pltpu.make_async_remote_copy(
            earlier.at[other], entering.at[ctx], out_b, in_b,
            device_id=(other, user), device_id_type=MESH,
        ).start()
    entering[ctx] = earlier[ctx]

    for w in range(positions // WIDE // 2, positions // WIDE):
        local(w)

    pltpu.make_async_copy(some, some, in_b).wait()
    pltpu.make_async_copy(some, some, out_b).wait()

    stores = []
    mean = jnp.full((HEAD, HEAD), 1.0 / HEAD, BF16)
    for c in range(chunks):
        at = pl.ds(c * CHUNK, CHUNK)
        heads = []
        for h in range(HEADS):
            s = slice(h * HEAD, (h + 1) * HEAD)
            n = HEAD // rows
            came = entering[h * n : (h + 1) * n].reshape(HEAD, HEAD).astype(F32)
            within = (state[c, h] + came).astype(BF16)
            mixed = intra[at, s] + jnp.dot(fq[at, s], within, preferred_element_type=F32)
            square = jnp.dot((mixed * mixed).astype(BF16), mean, preferred_element_type=F32)
            heads.append((mixed * lax.rsqrt(square + 1e-6) * scale[at, s]).astype(BF16))
        gated[at] = jnp.concatenate(heads, axis=1)
        stores.append(pltpu.make_async_copy(gated.at[at], out_hbm.at[at], stored.at[c]))
        stores[c].start()
    for store in stores:
        store.wait()
    some = req.at[pl.ds(0, devices - 1)]
    pltpu.make_async_copy(some, some, req_out).wait()
    some = send.at[pl.ds(0, devices - 1)]
    pltpu.make_async_copy(some, some, row_out).wait()


def encoder(owner, slot, table, wq, wk, wv, wg, gain):
    ctx_size = lax.axis_size("ctx")
    devices = ctx_size * lax.axis_size("user")
    groups = devices // GROUP
    parts, positions = owner.shape
    block = table.shape[1]
    width = wq.shape[1]
    args = (owner, slot, table, wq, wk, wv, wg, gain)
    requests = pltpu.VMEM((devices, 128), jnp.int32)
    whole = pltpu.VMEM((positions, width), BF16)
    piece = pltpu.VMEM((ctx_size, HEADS * HEAD // ctx_size, HEAD), BF16)
    one, many = pltpu.SemaphoreType.DMA, pltpu.SemaphoreType.DMA((groups,))
    return pl.pallas_call(
        encoder_kernel,
        out_shape=jax.ShapeDtypeStruct((positions, width), BF16),
        in_specs=[pl.BlockSpec(memory_space=pltpu.HBM)] * len(args),
        out_specs=pl.BlockSpec(memory_space=pltpu.HBM),
        scratch_shapes=[pltpu.VMEM(a.shape, a.dtype) for a in args]
        + [
            pltpu.VMEM((parts * positions // 128, 128), jnp.int32),
            pltpu.SMEM((parts * positions // 128, 128), jnp.int32),
            requests, requests,
            pltpu.SMEM((devices, 128), jnp.int32),
            pltpu.VMEM(table.shape, F32),
            pltpu.VMEM((CAP, block), F32),
            pltpu.VMEM((devices, CAP, block), BF16),
            pltpu.VMEM((devices, CAP, block), BF16),
            pltpu.VMEM((devices * CAP, block), F32),
            pltpu.VMEM((parts, positions, block), F32),
            whole, whole, whole, whole, whole,
            pltpu.VMEM((positions, width), F32),
            pltpu.VMEM((positions, width), F32),
            pltpu.VMEM((positions // CHUNK, HEADS, HEAD, HEAD), F32),
            piece, piece, piece, piece,
            pltpu.SemaphoreType.DMA((len(args),)),
            pltpu.SemaphoreType.DMA((positions // CHUNK,)),
            one, pltpu.SemaphoreType.REGULAR, one, many, many, one, many, one, one, one, one,
        ],
        compiler_params=pltpu.CompilerParams(
            collective_id=0, has_side_effects=True, vmem_limit_bytes=56 << 20
        ),
        name="encoder",
    )(*args)


def shards(
    robe_array, block_owner, block_slot, w_query, w_key, w_value, w_gate, w_output, head_gain
):
    owner = jnp.swapaxes(block_owner[0], 0, 1)
    slot = jnp.swapaxes(block_slot[0], 0, 1)
    gated = encoder(
        owner, slot, robe_array, w_query, w_key, w_value, w_gate, head_gain.reshape(1, -1)
    )
    encoded = jnp.dot(gated, w_output, preferred_element_type=F32).astype(BF16)
    return encoded[None]


def solution(mesh):
    return jax.shard_map(
        shards,
        mesh=mesh,
        in_specs=(
            P(("ctx", "user"), None),
            P("user", "ctx", None),
            P("user", "ctx", None),
            P(),
            P(),
            P(),
            P(),
            P(),
            P(),
        ),
        out_specs=P("user", "ctx", None),
        check_vma=False,
    )
```

```python
import jax
import jax.numpy as jnp
from jax import lax
from jax.experimental import pallas as pl
from jax.experimental.pallas import tpu as pltpu
from jax.sharding import PartitionSpec as P

MESH = pl.DeviceIdType.MESH
HEADS = 4
HEAD = 128
CAP = 80
GROUP = 16
CHUNK = 256
WIDE = 512
F32 = jnp.float32
BF16 = jnp.bfloat16


def moved(k, sign):
    c, y = lax.axis_index("ctx"), lax.axis_index("user")
    core, r = k % 2, k // 2
    a, b, e = r % 4, (r // 4) % 4, r // 16
    z = (c // 8 + 8 + sign * (a + b + e)) % 4
    x = ((c // 2) % 4 + 8 + sign * a) % 4
    u = (y + 8 + sign * (a + b)) % 4
    return z * 8 + x * 2 + (c + core) % 2, u


def encoder_kernel(
    own_hbm, slot_hbm, table_hbm, wq_hbm, wk_hbm, wv_hbm, wg_hbm, gain_hbm, out_hbm,
    own_ref, slot_ref, packed, wq_ref, wk_ref, wv_ref, wg_ref, gain_ref,
    ranked, index_ref, req, landed, arrived, table, gathered, send, recv, rows_ref,
    embed, items, gated, fq, fk, values, scale, intra, state, parcel, from_each, earlier, entering,
    loaded, stored, index_in, all_in, req_out, req_in, read_in, row_out, row_in, out_a, in_a, out_b, in_b,
):
    devices = send.shape[0]
    groups = devices // GROUP
    users = lax.axis_size("user")
    me = lax.axis_index("ctx") * users + lax.axis_index("user")
    ctx, user = lax.axis_index("ctx"), lax.axis_index("user")
    lane_size = users * 2
    chips = devices // lane_size
    chip, lane = ctx // 2, ctx % 2 * users + user
    same_lane = [(((chip + k) % chips) * 2 + ctx % 2, user) for k in range(chips)]
    lanes = [(lane + k) % lane_size for k in range(lane_size)]
    same_chip = [(chip * 2 + q // users, q % users) for q in lanes]
    barrier = pltpu.get_barrier_semaphore()
    for peer in same_lane[1:] + same_chip[1:]:
        pl.semaphore_signal(barrier, inc=1, device_id=peer, device_id_type=MESH)

    loads = [
        pltpu.make_async_copy(source, target, loaded.at[n])
        for n, (source, target) in enumerate(
            (
                (own_hbm, own_ref), (slot_hbm, slot_ref), (table_hbm, packed),
                (wk_hbm, wk_ref), (wv_hbm, wv_ref), (wq_hbm, wq_ref), (wg_hbm, wg_ref),
                (gain_hbm, gain_ref),
            )
        )
    ]
    for load in loads:
        load.start()
    loads[0].wait()
    loads[1].wait()

    parts, positions = own_ref.shape
    device_row = lax.broadcasted_iota(jnp.int32, (devices, CHUNK), 0)
    rank_row = lax.broadcasted_iota(jnp.int32, (128, CHUNK), 0)
    upper = jnp.where(
        lax.broadcasted_iota(jnp.int32, (CHUNK, CHUNK), 0)
        <= lax.broadcasted_iota(jnp.int32, (CHUNK, CHUNK), 1),
        1.0, 0.0,
    ).astype(BF16)
    before = jnp.zeros((devices, 1), F32)
    total = jnp.zeros((devices, 256), F32)
    for j in range(parts):
        for p in range(0, positions, CHUNK):
            if j == parts - 1 and p == 0:
                pl.semaphore_wait(barrier, chips + lane_size - 2)
                for peer in same_chip[1:]:
                    pl.semaphore_signal(all_in, inc=1, device_id=peer, device_id_type=MESH)
            own = own_ref[j : j + 1, p : p + CHUNK]
            slot = slot_ref[j : j + 1, p : p + CHUNK]
            named = device_row == own
            hot = jnp.where(named, 1.0, 0.0).astype(BF16)
            count = jnp.dot(hot, upper, preferred_element_type=F32) + before
            before = count[:, CHUNK - 1 :]
            rank = jnp.sum(jnp.where(named, count, 0.0), axis=0, keepdims=True).astype(jnp.int32) - 1
            spot = jnp.minimum(jnp.maximum(own * CAP + rank, 0), devices * CAP - 1)
            for b in range(CHUNK // 128):
                row = (j * positions + p) // 128 + b
                ranked[row : row + 1] = spot[:, b * 128 : (b + 1) * 128]
            at_rank = rank_row == rank
            high = jnp.where(at_rank, (slot >> 6).astype(F32), 0.0).astype(BF16)
            low = jnp.where(at_rank, (slot & 63).astype(F32), 0.0).astype(BF16)
            total += lax.dot_general(
                hot, jnp.concatenate([high, low], axis=0), (((1,), (1,)), ((), ())),
                preferred_element_type=F32,
            )
    asked = (total[:, :128] * 64.0 + total[:, 128:]).astype(jnp.int32)
    req[...] = jnp.minimum(jnp.maximum(asked, 0), table.shape[0] - 1)
    landed[pl.ds(0, 1)] = req[pl.ds(me, 1)]
    place = pltpu.make_async_copy(ranked, index_ref, index_in)
    place.start()

    loads[2].wait()

    def widen(k, carry):
        s = pl.ds(pl.multiple_of(k * 256, 256), 256)
        table[s] = packed[s].astype(F32)
        return carry

    lax.fori_loop(0, table.shape[0] // 256, widen, 0)
    pl.semaphore_wait(all_in, lane_size - 1)

    def ask(k, carry):
        ctx, user = moved(k, 1)
        pltpu.make_async_remote_copy(
            req.at[pl.ds(ctx * users + user, 1)], landed.at[pl.ds(k, 1)], req_out,
            req_in.at[k // GROUP], device_id=(ctx, user), device_id_type=MESH,
        ).start()
        return carry

    lax.fori_loop(1, devices, ask, 0, unroll=True)

    def read(g):
        some = landed.at[pl.ds(g * GROUP, GROUP)]
        return pltpu.make_async_copy(some, arrived.at[pl.ds(g * GROUP, GROUP)], read_in.at[g])

    def come(g):
        some = req.at[pl.ds(0, GROUP - (1 if g == 0 else 0))]
        pltpu.make_async_copy(some, some, req_in.at[g]).wait()
        read(g).start()

    def gather(k):
        for i in range(CAP):
            gathered[pl.ds(i, 1)] = table[pl.ds(arrived[k, i], 1)]
        return gathered[...].astype(BF16)

    def answer(k, carry):
        send[k] = gather(k)
        pltpu.make_async_remote_copy(
            send.at[k], recv.at[me], row_out, row_in.at[k // GROUP],
            device_id=moved(k, -1), device_id_type=MESH,
        ).start()
        return carry

    come(0)
    for g in range(groups):
        if g + 1 < groups:
            come(g + 1)
        read(g).wait()
        lax.fori_loop(g * GROUP + (1 if g == 0 else 0), (g + 1) * GROUP, answer, 0)
    recv[me] = gather(0)

    def unpack(k, carry):
        ctx, user = moved(k, 1)
        owner = ctx * users + user
        s = pl.ds(pl.multiple_of(owner * CAP, CAP), CAP)
        rows_ref[s] = recv[owner].astype(F32)
        return carry

    for g in range(groups):
        some = recv.at[pl.ds(0, GROUP - (1 if g == 0 else 0))]
        pltpu.make_async_copy(some, some, row_in.at[g]).wait()
        lax.fori_loop(g * GROUP, (g + 1) * GROUP, unpack, 0)
    ctx_size = lax.axis_size("ctx")
    chunks = positions // CHUNK

    place.wait()

    blocks = positions // 128

    def collect(b, carry):
        for i in range(128):
            for j in range(parts):
                row = rows_ref[pl.ds(index_ref[j * blocks + b, i], 1)]
                embed[j, pl.ds(b * 128 + i, 1)] = row
        return carry

    lax.fori_loop(0, blocks, collect, 0)

    for load in loads[3:]:
        load.wait()

    def feature(v):
        v = v.astype(BF16).astype(F32)
        return jnp.where(v > 0, v + 1.0, jnp.exp(jnp.minimum(v, 0.0))).astype(BF16)

    running = [jnp.zeros((HEAD, HEAD), F32)] * HEADS
    for w in range(positions // WIDE):
        at = pl.ds(w * WIDE, WIDE)
        e = jnp.concatenate([embed[j, at] for j in range(parts)], axis=1).astype(BF16)
        items[at] = e
        k = feature(jnp.dot(e, wk_ref[...], preferred_element_type=F32))
        v = jnp.dot(e, wv_ref[...], preferred_element_type=F32).astype(BF16)
        fk[at] = k
        values[at] = v
        for n in range(WIDE // CHUNK):
            r = slice(n * CHUNK, (n + 1) * CHUNK)
            for h in range(HEADS):
                s = slice(h * HEAD, (h + 1) * HEAD)
                state[w * (WIDE // CHUNK) + n, h] = running[h]
                running[h] = running[h] + lax.dot_general(
                    k[r, s], v[r, s], (((0,), (0,)), ((), ())), preferred_element_type=F32
                )
    rows = HEADS * HEAD // ctx_size
    for h in range(HEADS):
        for i in range(HEAD // rows):
            parcel[h * (HEAD // rows) + i] = running[h][i * rows : (i + 1) * rows].astype(BF16)

    ways = [(dz, dx, dc) for dz in range(4) for dx in range(4) for dc in range(2)]
    ways.sort(key=lambda w: -(min(w[0], 4 - w[0]) + min(w[1], 4 - w[1]) + 0.1 * w[2]))
    others = [
        (ctx // 8 + dz) % 4 * 8 + (ctx // 2 + dx) % 4 * 2 + (ctx + dc) % 2
        for dz, dx, dc in ways[:-1]
    ]
    for other in others:
        pltpu.make_async_remote_copy(
            parcel.at[other], from_each.at[ctx], out_a, in_a,
            device_id=(other, user), device_id_type=MESH,
        ).start()
    from_each[ctx] = parcel[ctx]

    causal = lax.broadcasted_iota(jnp.int32, (CHUNK, CHUNK), 0) >= lax.broadcasted_iota(
        jnp.int32, (CHUNK, CHUNK), 1
    )

    def local(w):
        whole = pl.ds(w * WIDE, WIDE)
        e = items[whole]
        q = feature(jnp.dot(e, wq_ref[...], preferred_element_type=F32))
        fq[whole] = q
        gate = jnp.dot(e, wg_ref[...], preferred_element_type=F32).astype(BF16).astype(F32)
        scale[whole] = gain_ref[...] * (gate / (1.0 + jnp.exp(-gate)))
        for n in range(WIDE // CHUNK):
            at = pl.ds(w * WIDE + n * CHUNK, CHUNK)
            for h in range(HEADS):
                s = slice(h * HEAD, (h + 1) * HEAD)
                scores = lax.dot_general(
                    q[n * CHUNK : (n + 1) * CHUNK, s], fk[at, s], (((1,), (1,)), ((), ())),
                    preferred_element_type=F32,
                )
                scores = jnp.where(causal, scores, 0.0).astype(BF16)
                intra[at, s] = jnp.dot(scores, values[at, s], preferred_element_type=F32)

    for w in range(positions // WIDE // 2):
        local(w)

    some = parcel.at[pl.ds(0, ctx_size - 1)]
    pltpu.make_async_copy(some, some, in_a).wait()
    sofar = jnp.zeros((rows, HEAD), F32)
    for i in range(ctx_size):
        earlier[i] = sofar.astype(BF16)
        sofar = sofar + from_each[i].astype(F32)

    for other in others:
        pltpu.make_async_remote_copy(
            earlier.at[other], entering.at[ctx], out_b, in_b,
            device_id=(other, user), device_id_type=MESH,
        ).start()
    entering[ctx] = earlier[ctx]

    for w in range(positions // WIDE // 2, positions // WIDE):
        local(w)

    pltpu.make_async_copy(some, some, in_b).wait()

    stores = []
    mean = jnp.full((HEAD, HEAD), 1.0 / HEAD, BF16)
    for c in range(chunks):
        at = pl.ds(c * CHUNK, CHUNK)
        heads = []
        for h in range(HEADS):
            s = slice(h * HEAD, (h + 1) * HEAD)
            n = HEAD // rows
            came = entering[h * n : (h + 1) * n].reshape(HEAD, HEAD).astype(F32)
            within = (state[c, h] + came).astype(BF16)
            mixed = intra[at, s] + jnp.dot(fq[at, s], within, preferred_element_type=F32)
            square = jnp.dot((mixed * mixed).astype(BF16), mean, preferred_element_type=F32)
            heads.append((mixed * lax.rsqrt(square + 1e-6) * scale[at, s]).astype(BF16))
        gated[at] = jnp.concatenate(heads, axis=1)
        stores.append(pltpu.make_async_copy(gated.at[at], out_hbm.at[at], stored.at[c]))
        stores[c].start()
    for store in stores:
        store.wait()
    some = parcel.at[pl.ds(0, ctx_size - 1)]
    pltpu.make_async_copy(some, some, out_a).wait()
    pltpu.make_async_copy(some, some, out_b).wait()
    some = req.at[pl.ds(0, devices - 1)]
    pltpu.make_async_copy(some, some, req_out).wait()
    some = send.at[pl.ds(0, devices - 1)]
    pltpu.make_async_copy(some, some, row_out).wait()


def encoder(owner, slot, table, wq, wk, wv, wg, gain):
    ctx_size = lax.axis_size("ctx")
    devices = ctx_size * lax.axis_size("user")
    groups = devices // GROUP
    parts, positions = owner.shape
    block = table.shape[1]
    width = wq.shape[1]
    args = (owner, slot, table, wq, wk, wv, wg, gain)
    requests = pltpu.VMEM((devices, 128), jnp.int32)
    whole = pltpu.VMEM((positions, width), BF16)
    piece = pltpu.VMEM((ctx_size, HEADS * HEAD // ctx_size, HEAD), BF16)
    one, many = pltpu.SemaphoreType.DMA, pltpu.SemaphoreType.DMA((groups,))
    return pl.pallas_call(
        encoder_kernel,
        out_shape=jax.ShapeDtypeStruct((positions, width), BF16),
        in_specs=[pl.BlockSpec(memory_space=pltpu.HBM)] * len(args),
        out_specs=pl.BlockSpec(memory_space=pltpu.HBM),
        scratch_shapes=[pltpu.VMEM(a.shape, a.dtype) for a in args]
        + [
            pltpu.VMEM((parts * positions // 128, 128), jnp.int32),
            pltpu.SMEM((parts * positions // 128, 128), jnp.int32),
            requests, requests,
            pltpu.SMEM((devices, 128), jnp.int32),
            pltpu.VMEM(table.shape, F32),
            pltpu.VMEM((CAP, block), F32),
            pltpu.VMEM((devices, CAP, block), BF16),
            pltpu.VMEM((devices, CAP, block), BF16),
            pltpu.VMEM((devices * CAP, block), F32),
            pltpu.VMEM((parts, positions, block), F32),
            whole, whole, whole, whole, whole,
            pltpu.VMEM((positions, width), F32),
            pltpu.VMEM((positions, width), F32),
            pltpu.VMEM((positions // CHUNK, HEADS, HEAD, HEAD), F32),
            piece, piece, piece, piece,
            pltpu.SemaphoreType.DMA((len(args),)),
            pltpu.SemaphoreType.DMA((positions // CHUNK,)),
            one, pltpu.SemaphoreType.REGULAR, one, many, many, one, many, one, one, one, one,
        ],
        compiler_params=pltpu.CompilerParams(
            collective_id=0, has_side_effects=True, vmem_limit_bytes=56 << 20
        ),
        name="encoder",
    )(*args)


def shards(
    robe_array, block_owner, block_slot, w_query, w_key, w_value, w_gate, w_output, head_gain
):
    owner = jnp.swapaxes(block_owner[0], 0, 1)
    slot = jnp.swapaxes(block_slot[0], 0, 1)
    gated = encoder(
        owner, slot, robe_array, w_query, w_key, w_value, w_gate, head_gain.reshape(1, -1)
    )
    encoded = jnp.dot(gated, w_output, preferred_element_type=F32).astype(BF16)
    return encoded[None]


def solution(mesh):
    return jax.shard_map(
        shards,
        mesh=mesh,
        in_specs=(
            P(("ctx", "user"), None),
            P("user", "ctx", None),
            P("user", "ctx", None),
            P(),
            P(),
            P(),
            P(),
            P(),
            P(),
        ),
        out_specs=P("user", "ctx", None),
        check_vma=False,
    )
```

```python
import jax
import jax.numpy as jnp
from jax import lax
from jax.experimental import pallas as pl
from jax.experimental.pallas import tpu as pltpu
from jax.sharding import PartitionSpec as P

MESH = pl.DeviceIdType.MESH
HEADS = 4
HEAD = 128
CAP = 80
GROUP = 16
CHUNK = 256
WIDE = 512
F32 = jnp.float32
BF16 = jnp.bfloat16


def moved(k, sign):
    c, y = lax.axis_index("ctx"), lax.axis_index("user")
    core, r = k % 2, k // 2
    a, b, e = r % 4, (r // 4) % 4, r // 16
    z = (c // 8 + 8 + sign * (a + b + e)) % 4
    x = ((c // 2) % 4 + 8 + sign * a) % 4
    u = (y + 8 + sign * (a + b)) % 4
    return z * 8 + x * 2 + (c + core) % 2, u


def encoder_kernel(
    own_hbm, slot_hbm, table_hbm, wq_hbm, wk_hbm, wv_hbm, wg_hbm, gain_hbm, out_hbm,
    own_ref, slot_ref, packed, wq_ref, wk_ref, wv_ref, wg_ref, gain_ref,
    ranked, index_ref, req, landed, arrived, table, gathered, send, recv, rows_ref,
    embed, items, gated, fq, fk, values, scale, intra, state, parcel, from_each, earlier, entering,
    loaded, stored, index_in, all_in, req_out, req_in, read_in, row_out, row_in, out_a, in_a, out_b, in_b,
):
    devices = send.shape[0]
    groups = devices // GROUP
    users = lax.axis_size("user")
    me = lax.axis_index("ctx") * users + lax.axis_index("user")
    ctx, user = lax.axis_index("ctx"), lax.axis_index("user")
    lane_size = users * 2
    chips = devices // lane_size
    chip, lane = ctx // 2, ctx % 2 * users + user
    same_lane = [(((chip + k) % chips) * 2 + ctx % 2, user) for k in range(chips)]
    lanes = [(lane + k) % lane_size for k in range(lane_size)]
    same_chip = [(chip * 2 + q // users, q % users) for q in lanes]
    barrier = pltpu.get_barrier_semaphore()
    for peer in same_lane[1:] + same_chip[1:]:
        pl.semaphore_signal(barrier, inc=1, device_id=peer, device_id_type=MESH)

    loads = [
        pltpu.make_async_copy(source, target, loaded.at[n])
        for n, (source, target) in enumerate(
            (
                (own_hbm, own_ref), (slot_hbm, slot_ref), (table_hbm, packed),
                (wk_hbm, wk_ref), (wv_hbm, wv_ref), (wq_hbm, wq_ref), (wg_hbm, wg_ref),
                (gain_hbm, gain_ref),
            )
        )
    ]
    for load in loads:
        load.start()
    loads[0].wait()
    loads[1].wait()

    parts, positions = own_ref.shape
    device_row = lax.broadcasted_iota(jnp.int32, (devices, CHUNK), 0)
    rank_row = lax.broadcasted_iota(jnp.int32, (128, CHUNK), 0)
    upper = jnp.where(
        lax.broadcasted_iota(jnp.int32, (CHUNK, CHUNK), 0)
        <= lax.broadcasted_iota(jnp.int32, (CHUNK, CHUNK), 1),
        1.0, 0.0,
    ).astype(BF16)
    before = jnp.zeros((devices, 1), F32)
    total = jnp.zeros((devices, 256), F32)
    for j in range(parts):
        for p in range(0, positions, CHUNK):
            if j == parts // 2 and p == 0:
                pl.semaphore_wait(barrier, chips + lane_size - 2)
                for peer in same_chip[1:]:
                    pl.semaphore_signal(all_in, inc=1, device_id=peer, device_id_type=MESH)
            own = own_ref[j : j + 1, p : p + CHUNK]
            slot = slot_ref[j : j + 1, p : p + CHUNK]
            named = device_row == own
            hot = jnp.where(named, 1.0, 0.0).astype(BF16)
            count = jnp.dot(hot, upper, preferred_element_type=F32) + before
            before = count[:, CHUNK - 1 :]
            rank = jnp.sum(jnp.where(named, count, 0.0), axis=0, keepdims=True).astype(jnp.int32) - 1
            spot = jnp.minimum(jnp.maximum(own * CAP + rank, 0), devices * CAP - 1)
            for b in range(CHUNK // 128):
                row = (j * positions + p) // 128 + b
                ranked[row : row + 1] = spot[:, b * 128 : (b + 1) * 128]
            at_rank = rank_row == rank
            high = jnp.where(at_rank, (slot >> 6).astype(F32), 0.0).astype(BF16)
            low = jnp.where(at_rank, (slot & 63).astype(F32), 0.0).astype(BF16)
            total += lax.dot_general(
                hot, jnp.concatenate([high, low], axis=0), (((1,), (1,)), ((), ())),
                preferred_element_type=F32,
            )
    asked = (total[:, :128] * 64.0 + total[:, 128:]).astype(jnp.int32)
    req[...] = jnp.minimum(jnp.maximum(asked, 0), table.shape[0] - 1)
    landed[pl.ds(0, 1)] = req[pl.ds(me, 1)]
    place = pltpu.make_async_copy(ranked, index_ref, index_in)
    place.start()

    loads[2].wait()

    def widen(k, carry):
        s = pl.ds(pl.multiple_of(k * 256, 256), 256)
        table[s] = packed[s].astype(F32)
        return carry

    lax.fori_loop(0, table.shape[0] // 256, widen, 0)
    pl.semaphore_wait(all_in, lane_size - 1)

    def ask(k, carry):
        ctx, user = moved(k, 1)
        pltpu.make_async_remote_copy(
            req.at[pl.ds(ctx * users + user, 1)], landed.at[pl.ds(k, 1)], req_out,
            req_in.at[k // GROUP], device_id=(ctx, user), device_id_type=MESH,
        ).start()
        return carry

    lax.fori_loop(1, devices, ask, 0, unroll=True)

    def read(g):
        some = landed.at[pl.ds(g * GROUP, GROUP)]
        return pltpu.make_async_copy(some, arrived.at[pl.ds(g * GROUP, GROUP)], read_in.at[g])

    def come(g):
        some = req.at[pl.ds(0, GROUP - (1 if g == 0 else 0))]
        pltpu.make_async_copy(some, some, req_in.at[g]).wait()
        read(g).start()

    def gather(k):
        for i in range(CAP):
            gathered[pl.ds(i, 1)] = table[pl.ds(arrived[k, i], 1)]
        return gathered[...].astype(BF16)

    def answer(k, carry):
        send[k] = gather(k)
        pltpu.make_async_remote_copy(
            send.at[k], recv.at[me], row_out, row_in.at[k // GROUP],
            device_id=moved(k, -1), device_id_type=MESH,
        ).start()
        return carry

    come(0)
    for g in range(groups):
        if g + 1 < groups:
            come(g + 1)
        read(g).wait()
        lax.fori_loop(g * GROUP + (1 if g == 0 else 0), (g + 1) * GROUP, answer, 0)
    recv[me] = gather(0)

    def unpack(k, carry):
        ctx, user = moved(k, 1)
        owner = ctx * users + user
        s = pl.ds(pl.multiple_of(owner * CAP, CAP), CAP)
        rows_ref[s] = recv[owner].astype(F32)
        return carry

    for g in range(groups):
        some = recv.at[pl.ds(0, GROUP - (1 if g == 0 else 0))]
        pltpu.make_async_copy(some, some, row_in.at[g]).wait()
        lax.fori_loop(g * GROUP, (g + 1) * GROUP, unpack, 0)
    ctx_size = lax.axis_size("ctx")
    chunks = positions // CHUNK

    place.wait()

    blocks = positions // 128

    def collect(b, carry):
        for i in range(128):
            for j in range(parts):
                row = rows_ref[pl.ds(index_ref[j * blocks + b, i], 1)]
                embed[j, pl.ds(b * 128 + i, 1)] = row
        return carry

    lax.fori_loop(0, blocks, collect, 0)

    for load in loads[3:]:
        load.wait()

    def feature(v):
        v = v.astype(BF16).astype(F32)
        return jnp.where(v > 0, v + 1.0, jnp.exp(jnp.minimum(v, 0.0))).astype(BF16)

    running = [jnp.zeros((HEAD, HEAD), F32)] * HEADS
    for w in range(positions // WIDE):
        at = pl.ds(w * WIDE, WIDE)
        e = jnp.concatenate([embed[j, at] for j in range(parts)], axis=1).astype(BF16)
        items[at] = e
        k = feature(jnp.dot(e, wk_ref[...], preferred_element_type=F32))
        v = jnp.dot(e, wv_ref[...], preferred_element_type=F32).astype(BF16)
        fk[at] = k
        values[at] = v
        for n in range(WIDE // CHUNK):
            r = slice(n * CHUNK, (n + 1) * CHUNK)
            for h in range(HEADS):
                s = slice(h * HEAD, (h + 1) * HEAD)
                state[w * (WIDE // CHUNK) + n, h] = running[h]
                running[h] = running[h] + lax.dot_general(
                    k[r, s], v[r, s], (((0,), (0,)), ((), ())), preferred_element_type=F32
                )
    rows = HEADS * HEAD // ctx_size
    for h in range(HEADS):
        for i in range(HEAD // rows):
            parcel[h * (HEAD // rows) + i] = running[h][i * rows : (i + 1) * rows].astype(BF16)

    ways = [(dz, dx, dc) for dz in range(4) for dx in range(4) for dc in range(2)]
    ways.sort(key=lambda w: -(min(w[0], 4 - w[0]) + min(w[1], 4 - w[1]) + 0.1 * w[2]))
    others = [
        (ctx // 8 + dz) % 4 * 8 + (ctx // 2 + dx) % 4 * 2 + (ctx + dc) % 2
        for dz, dx, dc in ways[:-1]
    ]
    for other in others:
        pltpu.make_async_remote_copy(
            parcel.at[other], from_each.at[ctx], out_a, in_a,
            device_id=(other, user), device_id_type=MESH,
        ).start()
    from_each[ctx] = parcel[ctx]

    causal = lax.broadcasted_iota(jnp.int32, (CHUNK, CHUNK), 0) >= lax.broadcasted_iota(
        jnp.int32, (CHUNK, CHUNK), 1
    )

    def local(w):
        whole = pl.ds(w * WIDE, WIDE)
        e = items[whole]
        q = feature(jnp.dot(e, wq_ref[...], preferred_element_type=F32))
        fq[whole] = q
        gate = jnp.dot(e, wg_ref[...], preferred_element_type=F32).astype(BF16).astype(F32)
        scale[whole] = gain_ref[...] * (gate / (1.0 + jnp.exp(-gate)))
        for n in range(WIDE // CHUNK):
            at = pl.ds(w * WIDE + n * CHUNK, CHUNK)
            for h in range(HEADS):
                s = slice(h * HEAD, (h + 1) * HEAD)
                scores = lax.dot_general(
                    q[n * CHUNK : (n + 1) * CHUNK, s], fk[at, s], (((1,), (1,)), ((), ())),
                    preferred_element_type=F32,
                )
                scores = jnp.where(causal, scores, 0.0).astype(BF16)
                intra[at, s] = jnp.dot(scores, values[at, s], preferred_element_type=F32)

    for w in range(positions // WIDE // 2):
        local(w)

    some = parcel.at[pl.ds(0, ctx_size - 1)]
    pltpu.make_async_copy(some, some, in_a).wait()
    sofar = jnp.zeros((rows, HEAD), F32)
    for i in range(ctx_size):
        earlier[i] = sofar.astype(BF16)
        sofar = sofar + from_each[i].astype(F32)

    for other in others:
        pltpu.make_async_remote_copy(
            earlier.at[other], entering.at[ctx], out_b, in_b,
            device_id=(other, user), device_id_type=MESH,
        ).start()
    entering[ctx] = earlier[ctx]

    for w in range(positions // WIDE // 2, positions // WIDE):
        local(w)

    pltpu.make_async_copy(some, some, in_b).wait()

    stores = []
    mean = jnp.full((HEAD, HEAD), 1.0 / HEAD, BF16)
    for c in range(chunks):
        at = pl.ds(c * CHUNK, CHUNK)
        heads = []
        for h in range(HEADS):
            s = slice(h * HEAD, (h + 1) * HEAD)
            n = HEAD // rows
            came = entering[h * n : (h + 1) * n].reshape(HEAD, HEAD).astype(F32)
            within = (state[c, h] + came).astype(BF16)
            mixed = intra[at, s] + jnp.dot(fq[at, s], within, preferred_element_type=F32)
            square = jnp.dot((mixed * mixed).astype(BF16), mean, preferred_element_type=F32)
            heads.append((mixed * lax.rsqrt(square + 1e-6) * scale[at, s]).astype(BF16))
        gated[at] = jnp.concatenate(heads, axis=1)
        stores.append(pltpu.make_async_copy(gated.at[at], out_hbm.at[at], stored.at[c]))
        stores[c].start()
    for store in stores:
        store.wait()
    some = parcel.at[pl.ds(0, ctx_size - 1)]
    pltpu.make_async_copy(some, some, out_a).wait()
    pltpu.make_async_copy(some, some, out_b).wait()
    some = req.at[pl.ds(0, devices - 1)]
    pltpu.make_async_copy(some, some, req_out).wait()
    some = send.at[pl.ds(0, devices - 1)]
    pltpu.make_async_copy(some, some, row_out).wait()


def encoder(owner, slot, table, wq, wk, wv, wg, gain):
    ctx_size = lax.axis_size("ctx")
    devices = ctx_size * lax.axis_size("user")
    groups = devices // GROUP
    parts, positions = owner.shape
    block = table.shape[1]
    width = wq.shape[1]
    args = (owner, slot, table, wq, wk, wv, wg, gain)
    requests = pltpu.VMEM((devices, 128), jnp.int32)
    whole = pltpu.VMEM((positions, width), BF16)
    piece = pltpu.VMEM((ctx_size, HEADS * HEAD // ctx_size, HEAD), BF16)
    one, many = pltpu.SemaphoreType.DMA, pltpu.SemaphoreType.DMA((groups,))
    return pl.pallas_call(
        encoder_kernel,
        out_shape=jax.ShapeDtypeStruct((positions, width), BF16),
        in_specs=[pl.BlockSpec(memory_space=pltpu.HBM)] * len(args),
        out_specs=pl.BlockSpec(memory_space=pltpu.HBM),
        scratch_shapes=[pltpu.VMEM(a.shape, a.dtype) for a in args]
        + [
            pltpu.VMEM((parts * positions // 128, 128), jnp.int32),
            pltpu.SMEM((parts * positions // 128, 128), jnp.int32),
            requests, requests,
            pltpu.SMEM((devices, 128), jnp.int32),
            pltpu.VMEM(table.shape, F32),
            pltpu.VMEM((CAP, block), F32),
            pltpu.VMEM((devices, CAP, block), BF16),
            pltpu.VMEM((devices, CAP, block), BF16),
            pltpu.VMEM((devices * CAP, block), F32),
            pltpu.VMEM((parts, positions, block), F32),
            whole, whole, whole, whole, whole,
            pltpu.VMEM((positions, width), F32),
            pltpu.VMEM((positions, width), F32),
            pltpu.VMEM((positions // CHUNK, HEADS, HEAD, HEAD), F32),
            piece, piece, piece, piece,
            pltpu.SemaphoreType.DMA((len(args),)),
            pltpu.SemaphoreType.DMA((positions // CHUNK,)),
            one, pltpu.SemaphoreType.REGULAR, one, many, many, one, many, one, one, one, one,
        ],
        compiler_params=pltpu.CompilerParams(
            collective_id=0, has_side_effects=True, vmem_limit_bytes=56 << 20
        ),
        name="encoder",
    )(*args)


def shards(
    robe_array, block_owner, block_slot, w_query, w_key, w_value, w_gate, w_output, head_gain
):
    owner = jnp.swapaxes(block_owner[0], 0, 1)
    slot = jnp.swapaxes(block_slot[0], 0, 1)
    gated = encoder(
        owner, slot, robe_array, w_query, w_key, w_value, w_gate, head_gain.reshape(1, -1)
    )
    encoded = jnp.dot(gated, w_output, preferred_element_type=F32).astype(BF16)
    return encoded[None]


def solution(mesh):
    return jax.shard_map(
        shards,
        mesh=mesh,
        in_specs=(
            P(("ctx", "user"), None),
            P("user", "ctx", None),
            P("user", "ctx", None),
            P(),
            P(),
            P(),
            P(),
            P(),
            P(),
        ),
        out_specs=P("user", "ctx", None),
        check_vma=False,
    )
```
